32 devices in a mesh: dp: 16 (over z, x, core), tensor: 2 (over y).
Axes of the slice: x: 2, y: 2, z: 4, core: 2. Of those that a mesh axis runs over, the one named last changes fastest.
Arguments:
- patches: bfloat16 [192, 64, 768], P('dp'), may hold values from -6 to 6
- visible: int32 [192], P('dp'), may hold values from 13 to 64, as said below
- cotangent: bfloat16 [192, 64, 768], P('dp'), may hold values from -6 to 6
- ln1_gain: float32 [768], replicated, may hold values from 0.5 to 1.5
- ln1_bias: float32 [768], replicated, may hold values from -3 to 3
- w_qkv: bfloat16 [3, 768, 768], P(None, 'dp', 'tensor'), may hold values from -0.21875 to 0.21875
- b_qkv: float32 [2, 768], P(None, 'tensor'), may hold values from -3 to 3
- w_out: bfloat16 [768, 768], P('tensor', 'dp'), may hold values from -0.875 to 0.875
- b_out: float32 [768], replicated, may hold values from -3 to 3
- ln2_gain: float32 [768], replicated, may hold values from 0.5 to 1.5
- ln2_bias: float32 [768], replicated, may hold values from -3 to 3
- w_up: bfloat16 [768, 3072], P('dp', 'tensor'), may hold values from -0.21875 to 0.21875
- b_up: float32 [3072], P('tensor'), may hold values from -3 to 3
- w_down: bfloat16 [3072, 768], P('tensor', 'dp'), may hold values from -0.109375 to 0.109375
- b_down: float32 [768], replicated, may hold values from -3 to 3
Outputs:
- block_output: bfloat16 [192, 64, 768], P('dp')
- patches_grad: bfloat16 [192, 64, 768], P('dp')
- ln1_gain_grad: float32 [768], replicated
- ln1_bias_grad: float32 [768], replicated
- w_qkv_grad: float32 [3, 768, 768], P(None, 'dp', 'tensor')
- b_qkv_grad: float32 [2, 768], P(None, 'tensor')
- w_out_grad: float32 [768, 768], P('tensor', 'dp')
- b_out_grad: float32 [768], replicated
- ln2_gain_grad: float32 [768], replicated
- ln2_bias_grad: float32 [768], replicated
- w_up_grad: float32 [768, 3072], P('dp', 'tensor')
- b_up_grad: float32 [3072], P('tensor')
- w_down_grad: float32 [3072, 768], P('tensor', 'dp')
- b_down_grad: float32 [768], replicated
The draws below stay inside these ranges and needn't reach their ends.
Inputs may be any that keep to these rules, and one draw needn't show every extreme that they name: visible[s] is the number of visible patches of sample s; some sample has exactly 64 and some exactly 13.
All inputs are finite; a program needn't handle non-finite values.
Results may differ from the reference program's by a relative error of at most 0.015.
Values may be sent and summed in bfloat16 or wider, within the bound.
No kernel may reach another device: no remote copies, remote signals or barrier semaphores. Data moves between devices by JAX's collectives and lax.ppermute only.
A program may use at most 128 MiB of HBM per device.

```python
import math
import jax
import jax.numpy as jnp
from jax import lax

D = 768
H = 12
HD = 64
FF = 3072
VIS = 64
LEAST = 13
SAMP_DEV = 12
SAMPLES = 192
N_DP = 16


def draw_visible(key, part):
    key = jax.random.fold_in(key, 7)
    keys_split = jax.random.split(key, 3)
    counts = jax.random.randint(keys_split[0], (SAMPLES,), LEAST, VIS + 1, dtype=jnp.int32)
    first_pick = jax.random.randint(keys_split[1], (), 0, SAMPLES, dtype=jnp.int32)
    second_pick = (first_pick + 1 + jax.random.randint(keys_split[2], (), 0, SAMPLES - 1, dtype=jnp.int32)) % SAMPLES
    position = jnp.arange(SAMPLES, dtype=jnp.int32)
    counts = jnp.where(position == first_pick, VIS, counts)
    return jnp.where(position == second_pick, LEAST, counts)


def spiked(array, stream_key, source, target, parts, factor):
    def block_of(dim):
        return (jnp.arange(array.shape[dim]) // (array.shape[dim] // parts)).reshape((-1,) + (1,) * (array.ndim - 1 - dim))

    one_side = jax.random.permutation(stream_key, parts)[block_of(target)]
    second = (block_of(target) + parts // 2) % parts
    return jnp.where((block_of(source) == one_side) | (block_of(source) == second), factor * array, array)


def block_levels(rng, extent, shards, smallest, largest):
    gain = 1.0
    for dim, blocks in shards:
        heights = jax.random.uniform(jax.random.fold_in(jax.random.fold_in(rng, 6), dim), (blocks,), jnp.float32, smallest / len(shards), largest / len(shards))
        gain = gain * jnp.repeat(jnp.exp(heights), extent[dim] // blocks).reshape((-1,) + (1,) * (len(extent) - 1 - dim))
    return gain


def noise(rng, extent, scale, reach, shards=(), kind=jnp.bfloat16):
    level = block_levels(rng, extent, shards, -0.22, 0.18) if shards else 1.0
    result = jax.random.normal(rng, extent, jnp.float32) * scale * level
    return jnp.minimum(jnp.maximum(result, -reach), reach).astype(kind)


def gaussian_with(rng, extent, deviation, limit, cuts, heavy, kind=jnp.bfloat16):
    array = deviation * jax.random.normal(rng, extent, jnp.float32)
    if cuts:
        array = array * block_levels(rng, extent, cuts, -0.22, 0.18)
    return jnp.clip(spiked(array, jax.random.fold_in(rng, 3), *heavy), -limit, limit).astype(kind)


def setup_inputs(seed: int = 0) -> dict:
    arg_keys = jax.random.split(jax.random.key(seed), 16)
    patches = noise(arg_keys[0], (SAMPLES, VIS, D), 1.0, 6.0, ((0, 16),))
    visible = draw_visible(jax.random.fold_in(arg_keys[15], 71), 0)
    cotangent = gaussian_with(arg_keys[2], (SAMPLES, VIS, D), 1.0, 6.0, ((0, 16),), (0, 2, 16, 2.0))
    ln1_gain = jnp.clip(1.0 + 0.1 * jax.random.normal(arg_keys[3], (D,), jnp.float32), 0.5, 1.5)
    ln1_bias = noise(arg_keys[4], (D,), 0.5, 3.0, (), jnp.float32)
    w_qkv = noise(arg_keys[5], (3, D, D), D ** -0.5, 0.21875, ((1, 16), (2, 2)))
    b_qkv = noise(arg_keys[6], (2, D), 0.5, 3.0, ((1, 2),), jnp.float32)
    w_out = noise(arg_keys[7], (D, D), (D // 16) ** -0.5, 0.875, ((0, 2), (1, 16)))
    b_out = noise(arg_keys[8], (D,), 0.5, 3.0, (), jnp.float32)
    ln2_gain = jnp.clip(1.0 + 0.1 * jax.random.normal(arg_keys[9], (D,), jnp.float32), 0.5, 1.5)
    ln2_bias = noise(arg_keys[10], (D,), 0.5, 3.0, (), jnp.float32)
    w_up = noise(arg_keys[11], (D, FF), D ** -0.5, 0.21875, ((0, 16), (1, 2)))
    b_up = noise(arg_keys[12], (FF,), 0.5, 3.0, ((0, 2),), jnp.float32)
    w_down = noise(arg_keys[13], (FF, D), FF ** -0.5, 0.109375, ((0, 2), (1, 16)))
    b_down = noise(arg_keys[14], (D,), 0.5, 3.0, (), jnp.float32)
    return {"patches": patches, "visible": visible, "cotangent": cotangent, "ln1_gain": ln1_gain, "ln1_bias": ln1_bias, "w_qkv": w_qkv, "b_qkv": b_qkv, "w_out": w_out, "b_out": b_out, "ln2_gain": ln2_gain, "ln2_bias": ln2_bias, "w_up": w_up, "b_up": b_up, "w_down": w_down, "b_down": b_down}


@jax.custom_vjp
def low(v):
    return lax.optimization_barrier(v.astype(jnp.bfloat16)).astype(jnp.float32)

@jax.custom_vjp
def low_back(v):
    return v

def low_keep(v):
    return (low(v), None)

def low_pass(kept, grad):
    return (grad,)

def back_keep(v):
    return (v, None)

def back_low(kept, grad):
    return (low(grad),)
low.defvjp(low_keep, low_pass)
low_back.defvjp(back_keep, back_low)
highest = lax.Precision.HIGHEST
norm_epsilon = 1e-06

def layer_norm(patch_rows, gain_row, bias_row):
    row_mean = lax.optimization_barrier(jnp.mean(patch_rows, axis=-1, keepdims=True))
    centred = patch_rows - row_mean
    spread = lax.optimization_barrier(jnp.mean(centred * centred, axis=-1, keepdims=True))
    return centred * lax.rsqrt(spread + norm_epsilon) * gain_row + bias_row

def product(left, right):
    return jnp.dot(left, right, precision=highest)

def attend(queries, key_rows, values, counts):
    head_shape = (SAMP_DEV, VIS, H, HD)
    raw_scores = jnp.einsum('sqhd,skhd->shqk', queries.reshape(head_shape), key_rows.reshape(head_shape), precision=highest)
    position = jnp.arange(VIS, dtype=jnp.int32)
    is_valid = position[None, :] < counts[:, None]
    scores = low_back(jnp.where(is_valid[:, None, None, :], raw_scores * (1.0 / math.sqrt(HD)), -1000000000.0))
    probabilities = low(jax.nn.softmax(scores, axis=-1))
    mixed_heads = jnp.einsum('shqk,skhd->sqhd', probabilities, values.reshape(head_shape), precision=highest)
    return mixed_heads.reshape(SAMP_DEV * VIS, H * HD)

def layer_forward(patch_rows, counts, ln1_gain, ln1_bias, w_qkv, b_qkv, w_out, b_out, ln2_gain, ln2_bias, w_up, b_up, w_down, b_down):
    normed = low(layer_norm(patch_rows, ln1_gain, ln1_bias))
    queries = low(low_back(product(normed, w_qkv[0]) + b_qkv[0]))
    key_rows = low(low_back(product(normed, w_qkv[1])))
    values = low(low_back(product(normed, w_qkv[2]) + b_qkv[1]))
    mixed_heads = low(low_back(attend(queries, key_rows, values, counts)))
    middle = patch_rows + low_back(product(mixed_heads, w_out) + b_out)
    hidden_in = low(layer_norm(middle, ln2_gain, ln2_bias))
    upper_pre = low_back(product(hidden_in, w_up) + b_up)
    active = low(jax.nn.gelu(upper_pre, approximate=False))
    return middle + low_back(product(active, w_down) + b_down)

def reference(patches, visible, cotangent, ln1_gain, ln1_bias, w_qkv, b_qkv, w_out, b_out, ln2_gain, ln2_bias, w_up, b_up, w_down, b_down):
    params = tuple((argument.astype(jnp.float32) for argument in (ln1_gain, ln1_bias, w_qkv, b_qkv, w_out, b_out, ln2_gain, ln2_bias, w_up, b_up, w_down, b_down)))
    grouped = (patches.reshape(N_DP, SAMP_DEV * VIS, D), visible.reshape(N_DP, SAMP_DEV), cotangent.reshape(N_DP, SAMP_DEV * VIS, D))

    def step_group(grad_totals, group_data):
        block_rows, counts, seed_rows = group_data

        def run_layer(patch_rows, *weights):
            return layer_forward(patch_rows, counts, *weights)
        output, pullback = jax.vjp(run_layer, block_rows.astype(jnp.float32), *params)
        gradients = pullback(seed_rows.astype(jnp.float32))
        grad_totals = jax.tree.map(jnp.add, grad_totals, tuple(gradients[1:]))
        return (grad_totals, (output.astype(jnp.bfloat16), gradients[0].astype(jnp.bfloat16)))
    zero_totals = tuple((jnp.zeros_like(argument) for argument in params))
    grad_totals, (outputs, input_grads) = lax.scan(step_group, zero_totals, grouped)
    return (outputs.reshape(SAMPLES, VIS, D), input_grads.reshape(SAMPLES, VIS, D), grad_totals[0], grad_totals[1], grad_totals[2], grad_totals[3], grad_totals[4], grad_totals[5], grad_totals[6], grad_totals[7], grad_totals[8], grad_totals[9], grad_totals[10], grad_totals[11])
```

```python
import functools

import jax
import jax.numpy as jnp
from jax import lax
from jax.experimental import pallas as pl
from jax.experimental.pallas import tpu as pltpu
from jax.sharding import PartitionSpec as P

HD = 64
VIS = 64
EPS = 1e-06
BF = jnp.bfloat16
F32 = jnp.float32
NEG = -1000000000.0
PAIR = 2 * VIS
VMEM_BYTES = 56 * 1024 * 1024

NN = (((1,), (0,)), ((), ()))
NT = (((1,), (1,)), ((), ()))
TN = (((0,), (0,)), ((), ()))


def mm(left, right, dims=NN):
    return lax.dot_general(left, right, dims, preferred_element_type=F32)


def rows_of(t):
    return pl.ds(t * PAIR, PAIR)


def norm_stats(v):
    mean = jnp.mean(v, axis=-1, keepdims=True)
    centred = v - mean
    inv = lax.rsqrt(jnp.mean(centred * centred, axis=-1, keepdims=True) + EPS)
    return centred * inv, inv


def low_lanes(shape):
    return lax.broadcasted_iota(jnp.int32, shape, 1) < HD


def two_heads(block, low):
    zero = jnp.zeros_like(block)
    return jnp.concatenate([jnp.where(low, block, zero), jnp.where(low, zero, block)], axis=0)


def col_sum(v):
    return jnp.sum(v, axis=0, keepdims=True)


def attend_kernel(base, n_alias, counts, x, gain, bias, w, b_q, b_v, *refs):
    norm_o, q_o, k_o, v_o, probs_o, mixed_o, proj_o = refs[n_alias:]
    rows, d = x.shape
    e = q_o.shape[1]
    for t in range(rows // PAIR):
        xhat, _ = norm_stats(x[rows_of(t), :].astype(F32))
        norm_o[rows_of(t), :] = (xhat * gain[...] + bias[...]).astype(BF)
    n = norm_o[...]
    q_o[...] = (mm(n, w[:, 0:e]) + b_q[...]).astype(BF)
    k_o[...] = mm(n, w[:, e : 2 * e]).astype(BF)
    v_o[...] = (mm(n, w[:, 2 * e : 3 * e]) + b_v[...]).astype(BF)
    low = low_lanes((PAIR, PAIR))
    row = lax.broadcasted_iota(jnp.int32, (PAIR, PAIR), 0)
    col = lax.broadcasted_iota(jnp.int32, (PAIR, PAIR), 1)
    pairs = e // PAIR
    for t in range(rows // PAIR):
        first = counts[base + 2 * t]
        second = counts[base + 2 * t + 1]
        valid = ((row < VIS) & (col < jnp.minimum(first, VIS))) | (
            (row >= VIS) & (col >= VIS) & (col < VIS + second)
        )
        for p in range(pairs):
            lanes = pl.ds(p * PAIR, PAIR)
            q2 = q_o[rows_of(t), lanes]
            kc = two_heads(k_o[rows_of(t), lanes], low)
            vc = two_heads(v_o[rows_of(t), lanes], low)
            scores = mm(q2, kc, NT) * (HD**-0.5)
            for h in range(2):
                s = jnp.where(valid, scores[:, h * PAIR : (h + 1) * PAIR], NEG)
                ex = jnp.exp(s - jnp.max(s, axis=-1, keepdims=True))
                probs_o[t * pairs + p, :, pl.ds(h * PAIR, PAIR)] = ex / jnp.sum(
                    ex, axis=-1, keepdims=True
                )
            pb = probs_o[t * pairs + p].astype(BF)
            mixed_o[rows_of(t), lanes] = mm(pb, vc).astype(BF)
    proj_o[...] = mm(mixed_o[...], w[:, 3 * e : 4 * e], NT).astype(BF)


def feed_kernel(
    n_alias, first, off, x, own, other, b_out, gain, bias, w_up, w_dn, b_up, cot, sums, *refs
):
    mid_o, norm_o, act_o, gu_o, down_o, gn_o, sums_o = refs[n_alias : n_alias + 7]
    down_acc, gn_acc = refs[n_alias + 7 :]
    rows, d = x.shape
    f = w_up.shape[1]
    up_at, down_at = off
    for t in range(rows // PAIR):
        r = rows_of(t)
        middle = x[r, :].astype(F32) + (
            (own[r, :].astype(F32) + other[r, :].astype(F32)) + b_out[...]
        )
        mid_o[r, :] = middle
        xhat, _ = norm_stats(middle)
        norm_o[r, :] = (xhat * gain[...] + bias[...]).astype(BF)
    if first:
        sums_o[...] = jnp.zeros_like(sums_o)
    else:
        sums_o[...] = sums[...]
    sums_o[:, down_at : down_at + d] += col_sum(cot[...].astype(F32))
    tile = 256
    for j in range(f // tile):
        c = pl.ds(j * tile, tile)
        u = mm(norm_o[...], w_up[:, c]) + b_up[:, c]
        ga = mm(cot[...], w_dn[:, c])
        cdf = 0.5 * (1.0 + lax.erf(u * (0.5**0.5)))
        pdf = jnp.exp(u * u * -0.5) * 0.3989422804014327
        act_o[:, c] = (u * cdf).astype(BF)
        gu = (ga * (cdf + u * pdf)).astype(BF)
        gu_o[:, c] = gu
        sums_o[:, up_at + j * tile : up_at + (j + 1) * tile] += col_sum(gu.astype(F32))
        gn = mm(gu, w_up[:, c], NT)
        dn = mm(act_o[:, c], w_dn[:, c], NT)
        if j == 0:
            gn_acc[...] = gn
            down_acc[...] = dn
        else:
            gn_acc[...] += gn
            down_acc[...] += dn
    gn_o[...] = gn_acc[...].astype(BF)
    down_o[...] = down_acc[...].astype(BF)


def back_kernel(
    n_alias, off, middle, own, other, cot, gain2, w, q, k, v, probs, x, sums, *refs
):
    gp_o, gm_o, gqkv_o, gn_o, sums_o = refs[n_alias : n_alias + 5]
    gmix = refs[n_alias + 5]
    rows, d = x.shape
    e = q.shape[1]
    sums_o[...] = sums[...]
    g1_at, b1_at, qv_at, out_at, g2_at, b2_at = off
    for t in range(rows // PAIR):
        r = rows_of(t)
        gn = own[r, :].astype(F32) + other[r, :].astype(F32)
        xhat, inv = norm_stats(middle[r, :])
        tt = gn * gain2[...]
        grad = cot[r, :].astype(F32) + inv * (
            tt
            - jnp.mean(tt, axis=-1, keepdims=True)
            - xhat * jnp.mean(tt * xhat, axis=-1, keepdims=True)
        )
        gm_o[r, :] = grad
        gp = grad.astype(BF)
        gp_o[r, :] = gp
        sums_o[:, g2_at : g2_at + d] += col_sum(gn * xhat)
        sums_o[:, b2_at : b2_at + d] += col_sum(gn)
        sums_o[:, out_at : out_at + d] += col_sum(gp.astype(F32))
    gmix[...] = mm(gp_o[...], w[:, 3 * e : 4 * e]).astype(BF)
    low = low_lanes((PAIR, PAIR))
    pairs = e // PAIR
    for t in range(rows // PAIR):
        r = rows_of(t)
        for p in range(pairs):
            lanes = pl.ds(p * PAIR, PAIR)
            q2 = q[r, lanes]
            g2 = gmix[r, lanes]
            kc = two_heads(k[r, lanes], low)
            vc = two_heads(v[r, lanes], low)
            pr = probs[t * pairs + p]
            gprob = mm(g2, vc, NT)
            prod = pr * gprob
            tot = jnp.concatenate(
                [
                    jnp.broadcast_to(
                        jnp.sum(prod[:, h * PAIR : (h + 1) * PAIR], axis=-1, keepdims=True),
                        (PAIR, PAIR),
                    )
                    for h in range(2)
                ],
                axis=1,
            )
            gs = (pr * (gprob - tot)).astype(BF)
            gq = mm(gs, kc) * (HD**-0.5)
            gk = mm(gs, q2, TN)
            gv = mm(pr.astype(BF), g2, TN)
            gqkv_o[r, pl.ds(p * PAIR, PAIR)] = gq.astype(BF)
            gqkv_o[r, pl.ds(e + p * PAIR, PAIR)] = (
                jnp.where(low, gk[:PAIR], gk[PAIR:]) * (HD**-0.5)
            ).astype(BF)
            gqkv_o[r, pl.ds(2 * e + p * PAIR, PAIR)] = jnp.where(
                low, gv[:PAIR], gv[PAIR:]
            ).astype(BF)
    sums_o[:, qv_at : qv_at + e] += col_sum(gqkv_o[:, 0:e].astype(F32))
    sums_o[:, qv_at + e : qv_at + 2 * e] += col_sum(gqkv_o[:, 2 * e : 3 * e].astype(F32))
    gn_o[...] = mm(gqkv_o[...], w[:, 0 : 3 * e], NT).astype(BF)
    for t in range(rows // PAIR):
        r = rows_of(t)
        xhat, _ = norm_stats(x[r, :].astype(F32))
        gn = gn_o[r, :].astype(F32)
        sums_o[:, g1_at : g1_at + d] += col_sum(gn * xhat)
        sums_o[:, b1_at : b1_at + d] += col_sum(gn)


def rows_kernel(n_alias, x, own, other, gm, gain, *refs):
    (out,) = refs[n_alias:]
    for t in range(x.shape[0] // PAIR):
        r = rows_of(t)
        gn = own[r, :].astype(F32) + other[r, :].astype(F32)
        xhat, inv = norm_stats(x[r, :].astype(F32))
        tt = gn * gain[...]
        out[r, :] = (
            gm[r, :]
            + inv
            * (
                tt
                - jnp.mean(tt, axis=-1, keepdims=True)
                - xhat * jnp.mean(tt * xhat, axis=-1, keepdims=True)
            )
        ).astype(BF)


def chunk_spec(shape, ch):
    return pl.BlockSpec(shape, lambda i: (ch,) + (0,) * (len(shape) - 1))


def whole_spec(shape):
    return pl.BlockSpec(shape, lambda i: (0,) * len(shape))


SMEM_SPEC = pl.BlockSpec(memory_space=pltpu.SMEM)


def call(kernel, ch, n_ch, inputs, kept, fresh, scratch=(), flops=0, name=None):
    in_specs, args = [], []
    for arr, kind in inputs:
        args.append(arr)
        if kind == "s":
            in_specs.append(SMEM_SPEC)
        elif kind == "c":
            in_specs.append(chunk_spec((arr.shape[0] // n_ch,) + arr.shape[1:], ch))
        else:
            in_specs.append(whole_spec(arr.shape))
    out_shapes, out_specs, aliases = [], [], {}
    for i, (shape, dtype, previous) in enumerate(kept):
        out_shapes.append(jax.ShapeDtypeStruct(shape, dtype))
        out_specs.append(chunk_spec((shape[0] // n_ch,) + shape[1:], ch))
        if previous is not None:
            aliases[len(args)] = i
            args.append(previous)
            in_specs.append(pl.BlockSpec(memory_space=pl.ANY))
    for shape, dtype in fresh:
        out_shapes.append(jax.ShapeDtypeStruct(shape, dtype))
        out_specs.append(whole_spec(shape))
    nbytes = sum(a.size * a.dtype.itemsize for a in args)
    return pl.pallas_call(
        functools.partial(kernel, len(aliases)),
        grid=(1,),
        in_specs=in_specs,
        out_specs=out_specs,
        out_shape=out_shapes,
        scratch_shapes=list(scratch),
        input_output_aliases=aliases,
        compiler_params=pltpu.CompilerParams(vmem_limit_bytes=VMEM_BYTES),
        cost_estimate=pl.CostEstimate(flops=flops, bytes_accessed=nbytes, transcendentals=0),
        name=name,
    )(*args)


def after(x, *deps):
    return lax.optimization_barrier((x,) + deps)[0]


class Links:
    def __init__(self, n):
        self.n = n
        self.depth = n // 4
        me = lax.axis_index("dp")
        self.core, self.x, self.z = me % 2, (me // 2) % 2, me // 4

    def core_swap(self, v):
        return lax.ppermute(v, "dp", [(i, i ^ 1) for i in range(self.n)])

    def x_swap(self, v):
        return lax.ppermute(v, "dp", [(i, i ^ 2) for i in range(self.n)])

    def z_shift(self, v, k):
        return lax.ppermute(v, "dp", [(i, (i + 4 * k) % self.n) for i in range(self.n)])

    def z_xor(self, v, k):
        return lax.ppermute(v, "dp", [(i, i ^ (4 * k)) for i in range(self.n)])


def y_swap(v):
    return lax.ppermute(v, "tensor", [(0, 1), (1, 0)])


def place_kernel(where, mine, others, out):
    z, x, c = where[0], where[1], where[2]
    depth = mine.shape[0] // 2
    for j in range(2 * depth):
        zz = lax.rem(z - (j % depth) + depth, depth)
        xx = x if j < depth else 1 - x
        base = (zz * 2 + xx) * 2
        out[base + c] = mine[j]
        out[base + 1 - c] = others[j]


def place(links, mine, others):
    n, (r, c) = links.n, mine.shape[1:]
    where = jnp.stack([links.z, links.x, links.core]).astype(jnp.int32)
    out = pl.pallas_call(
        place_kernel,
        grid=(1,),
        in_specs=[SMEM_SPEC, whole_spec(mine.shape), whole_spec(mine.shape)],
        out_specs=whole_spec((n, r, c)),
        out_shape=jax.ShapeDtypeStruct((n, r, c), mine.dtype),
        compiler_params=pltpu.CompilerParams(vmem_limit_bytes=VMEM_BYTES),
        cost_estimate=pl.CostEstimate(flops=0, bytes_accessed=4 * mine.size * 2, transcendentals=0),
        name="place",
    )(where, mine, others)
    return out.reshape(n * r, c)


def gather_z(links, own):
    return [links.z_shift(own, k) for k in range(1, links.depth)]


def gather_rest(links, own, received, x_own=None):
    if x_own is None:
        stack = jnp.stack([own] + received)
        mine = jnp.concatenate([stack, links.x_swap(stack)])
    else:
        stack = jnp.stack(received)
        mine = jnp.concatenate([own[None], stack, x_own[None], links.x_swap(stack)])
    return place(links, mine, links.core_swap(mine))


def scatter(links, grad):
    n, depth = links.n, links.depth
    d, c = grad.shape
    g = grad.reshape(n // 2, 2, d // n, c)
    pick = functools.partial(lax.dynamic_index_in_dim, axis=1, keepdims=False)
    got = links.core_swap(pick(g, 1 - links.core))
    total = (pick(g, links.core).astype(F32) + got.astype(F32)).astype(BF)
    g = total.reshape(depth, 2, d // n, c)
    got = links.x_swap(pick(g, 1 - links.x))
    total = pick(g, links.x).astype(F32) + got.astype(F32)
    pick = functools.partial(lax.dynamic_index_in_dim, axis=0, keepdims=False)
    send = total.astype(BF)
    parts = [
        links.z_shift(pick(send, lax.rem(links.z + k, depth)), k) for k in range(1, depth)
    ]
    result = pick(total, links.z)
    for part in parts:
        result = result + part.astype(F32)
    return result


def sum_dp(links, v):
    v = v + links.core_swap(v)
    v = v + links.x_swap(v)
    v = v + links.z_xor(v, 1)
    return v + links.z_xor(v, 2)


def local(
    n_dp,
    patches,
    visible,
    cotangent,
    ln1_gain,
    ln1_bias,
    w_qkv,
    b_qkv,
    w_out,
    b_out,
    ln2_gain,
    ln2_bias,
    w_up,
    b_up,
    w_down,
    b_down,
):
    samples, vis, d = patches.shape
    rows = samples * vis
    e = w_qkv.shape[2]
    f = w_up.shape[1]
    n_ch = 2
    per = rows // n_ch
    fast = n_dp == 16
    links = Links(n_dp)

    own_att = jnp.concatenate([w_qkv[0], w_qkv[1], w_qkv[2], w_out.T], axis=1)
    own_dn = w_down.T
    if fast:
        z_att = gather_z(links, own_att)
        x_att = links.x_swap(own_att)
        w_att = gather_rest(links, own_att, z_att, x_att)
        z_up = gather_z(links, after(w_up, *z_att))
        w_upf = gather_rest(links, w_up, z_up)
        z_dn = gather_z(links, after(own_dn, *z_up))
        w_dnf = gather_rest(links, own_dn, z_dn)
    else:
        w_att, w_upf, w_dnf = (
            lax.all_gather(w, "dp", axis=0, tiled=True) for w in (own_att, w_up, own_dn)
        )

    x = patches.reshape(rows, d)
    cot = cotangent.reshape(rows, d)
    row = lambda v: v.reshape(1, -1)
    groups = rows // PAIR * (e // PAIR)

    at = [0]
    for size in (d, d, e, e, d, d, d, f, d):
        at.append(at[-1] + size)
    n_sums = at[-1]

    kept = [None] * 6
    proj = []
    for ch in range(n_ch):
        *kept, out = call(
            functools.partial(attend_kernel, ch * (samples // n_ch)),
            ch,
            n_ch,
            [
                (visible, "s"),
                (x, "c"),
                (row(ln1_gain), "w"),
                (row(ln1_bias), "w"),
                (w_att, "w"),
                (row(b_qkv[0]), "w"),
                (row(b_qkv[1]), "w"),
            ],
            [
                ((rows, d), BF, kept[0]),
                ((rows, e), BF, kept[1]),
                ((rows, e), BF, kept[2]),
                ((rows, e), BF, kept[3]),
                ((groups, PAIR, 2 * PAIR), F32, kept[4]),
                ((rows, e), BF, kept[5]),
            ],
            [((per, d), BF)],
            flops=2 * per * d * 4 * e,
            name=f"attend{ch}",
        )
        proj.append(out)
    norm1, q, k, v, probs, mixed = kept
    proj_got = []
    for ch in range(n_ch):
        proj_got.append(y_swap(proj[ch] if ch == 0 else after(proj[ch], proj_got[-1])))

    kept = [None] * 4
    down, gn2 = [], []
    sums = jnp.zeros((1, n_sums), F32)
    for ch in range(n_ch):
        *kept, down_c, gn_c, sums = call(
            lambda n_alias, *refs, ch=ch: feed_kernel(n_alias, ch == 0, (at[7], at[8]), *refs),
            ch,
            n_ch,
            [
                (x, "c"),
                (proj[ch], "w"),
                (proj_got[ch], "w"),
                (row(b_out), "w"),
                (row(ln2_gain), "w"),
                (row(ln2_bias), "w"),
                (w_upf, "w"),
                (w_dnf, "w"),
                (row(b_up), "w"),
                (cot, "c"),
                (sums, "w"),
            ],
            [
                ((rows, d), F32, kept[0]),
                ((rows, d), BF, kept[1]),
                ((rows, f), BF, kept[2]),
                ((rows, f), BF, kept[3]),
            ],
            [((per, d), BF), ((per, d), BF), ((1, n_sums), F32)],
            scratch=[pltpu.VMEM((per, d), F32), pltpu.VMEM((per, d), F32)],
            flops=2 * per * d * 4 * f,
            name=f"feed{ch}",
        )
        down.append(down_c)
        gn2.append(gn_c)
    middle, norm2, active, grad_up = kept
    gn2_got = []
    for ch in range(n_ch):
        gn2_got.append(y_swap(gn2[ch] if ch == 0 else after(gn2[ch], gn2_got[-1])))
    down_got = []
    for ch in range(n_ch):
        down_got.append(y_swap(after(down[ch], gn2_got[-1], *down_got)))

    g_dn = mm(cot, active, TN).astype(BF)
    g_up = mm(norm2, grad_up, TN).astype(BF)

    kept = [None] * 3
    gn1 = []
    for ch in range(n_ch):
        *kept, gn_c, sums = call(
            lambda n_alias, *refs: back_kernel(
                n_alias, (at[0], at[1], at[2], at[4], at[5], at[6]), *refs
            ),
            ch,
            n_ch,
            [
                (middle, "c"),
                (gn2[ch], "w"),
                (gn2_got[ch], "w"),
                (cot, "c"),
                (row(ln2_gain), "w"),
                (w_att, "w"),
                (q, "c"),
                (k, "c"),
                (v, "c"),
                (probs, "c"),
                (x, "c"),
                (sums, "w"),
            ],
            [((rows, d), BF, kept[0]), ((rows, d), F32, kept[1]), ((rows, 3 * e), BF, kept[2])],
            [((per, d), BF), ((1, n_sums), F32)],
            scratch=[pltpu.VMEM((per, e), BF)],
            flops=2 * per * d * 4 * e,
            name=f"back{ch}",
        )
        gn1.append(gn_c)
    grad_proj, grad_mid, grad_qkv = kept
    gn1_got = []
    for ch in range(n_ch):
        gn1_got.append(y_swap(gn1[ch] if ch == 0 else after(gn1[ch], gn1_got[-1])))

    g_att = jnp.concatenate(
        [mm(norm1, grad_qkv, TN).astype(BF), mm(grad_proj, mixed, TN).astype(BF)], axis=1
    )
    if fast:
        s_dn = scatter(links, g_dn)
        s_up = scatter(links, g_up)
        s_att = scatter(links, g_att)
        sums = sum_dp(links, sums)
    else:
        s_dn, s_up, s_att = (
            lax.psum_scatter(g, "dp", scatter_dimension=0, tiled=True).astype(F32)
            for g in (g_dn, g_up, g_att)
        )
        sums = lax.psum(sums, "dp")
    ln1_sums = sums[:, : 2 * d] + y_swap(sums[:, : 2 * d])

    grad_rows = None
    for ch in range(n_ch):
        (grad_rows,) = call(
            rows_kernel,
            ch,
            n_ch,
            [
                (x, "c"),
                (gn1[ch], "w"),
                (gn1_got[ch], "w"),
                (grad_mid, "c"),
                (row(ln1_gain), "w"),
            ],
            [((rows, d), BF, grad_rows)],
            [],
            name=f"rows{ch}",
        )

    down_all = jnp.concatenate(
        [a.astype(F32) + b.astype(F32) for a, b in zip(down, down_got)], axis=0
    )
    output = (middle + (down_all + b_down)).astype(BF)

    flat = sums[0]
    part = lambda i: flat[at[i] : at[i + 1]]
    return (
        output.reshape(patches.shape),
        grad_rows.reshape(patches.shape),
        ln1_sums[0, :d],
        ln1_sums[0, d:],
        jnp.stack([s_att[:, 0:e], s_att[:, e : 2 * e], s_att[:, 2 * e : 3 * e]]),
        jnp.stack([part(2), part(3)]),
        s_att[:, 3 * e : 4 * e].T,
        part(4),
        part(5),
        part(6),
        s_up,
        part(7),
        s_dn.T,
        part(8),
    )


def solution(mesh):
    return jax.shard_map(
        functools.partial(local, mesh.shape["dp"]),
        mesh=mesh,
        in_specs=(
            P("dp", None, None),
            P("dp"),
            P("dp", None, None),
            P(),
            P(),
            P(None, "dp", "tensor"),
            P(None, "tensor"),
            P("tensor", "dp"),
            P(),
            P(),
            P(),
            P("dp", "tensor"),
            P("tensor"),
            P("tensor", "dp"),
            P(),
        ),
        out_specs=(
            P("dp", None, None),
            P("dp", None, None),
            P(),
            P(),
            P(None, "dp", "tensor"),
            P(None, "tensor"),
            P("tensor", "dp"),
            P(),
            P(),
            P(),
            P("dp", "tensor"),
            P("tensor"),
            P("tensor", "dp"),
            P(),
        ),
        check_vma=False,
    )
```

```python
import functools

import jax
import jax.numpy as jnp
from jax import lax
from jax.experimental import pallas as pl
from jax.experimental.pallas import tpu as pltpu
from jax.sharding import PartitionSpec as P

HD = 64
VIS = 64
EPS = 1e-06
BF = jnp.bfloat16
F32 = jnp.float32
NEG = -1000000000.0
PAIR = 2 * VIS
MIB = 1024 * 1024

NN = (((1,), (0,)), ((), ()))
NT = (((1,), (1,)), ((), ()))
TN = (((0,), (0,)), ((), ()))


def mm(left, right, dims=NN):
    return lax.dot_general(left, right, dims, preferred_element_type=F32)


def rows_of(t):
    return pl.ds(t * PAIR, PAIR)


def norm_stats(v):
    mean = jnp.mean(v, axis=-1, keepdims=True)
    centred = v - mean
    inv = lax.rsqrt(jnp.mean(centred * centred, axis=-1, keepdims=True) + EPS)
    return centred * inv, inv


def low_lanes(shape):
    return lax.broadcasted_iota(jnp.int32, shape, 1) < HD


def two_heads(block, low):
    zero = jnp.zeros_like(block)
    return jnp.concatenate([jnp.where(low, block, zero), jnp.where(low, zero, block)], axis=0)


def col_sum(v):
    return jnp.sum(v, axis=0, keepdims=True)


def weights(refs):
    if refs[0].shape != (3,):
        return refs[0], refs[1:]
    where, parts, buf = refs[0], refs[1:5], refs[-1]
    depth, r, _ = parts[0].shape
    for zz in range(depth):
        for i, part in enumerate(parts):
            xx = where[1] if i % 2 == 0 else 1 - where[1]
            cc = where[2] if i < 2 else 1 - where[2]
            start = pl.multiple_of(((zz * 2 + xx) * 2 + cc) * r, 16)
            buf[pl.ds(start, r), :] = part[zz]
    return buf, refs[5:-1]


def attend_kernel(base, at, n_alias, counts, x, small, *refs):
    w, refs = weights(refs)
    gain, bias, b_q, b_v = (small.at[:, at[i] : at[i + 1]] for i in (0, 1, 2, 3))
    norm_o, q_o, k_o, v_o, probs_o, mixed_o, proj_o = refs[n_alias : n_alias + 7]
    rows, d = x.shape
    e = q_o.shape[1]
    for t in range(rows // PAIR):
        xhat, _ = norm_stats(x[rows_of(t), :].astype(F32))
        norm_o[rows_of(t), :] = (xhat * gain[...] + bias[...]).astype(BF)
    n = norm_o[...]
    q_o[...] = (mm(n, w[:, 0:e]) + b_q[...]).astype(BF)
    k_o[...] = mm(n, w[:, e : 2 * e]).astype(BF)
    v_o[...] = (mm(n, w[:, 2 * e : 3 * e]) + b_v[...]).astype(BF)
    low = low_lanes((PAIR, PAIR))
    row = lax.broadcasted_iota(jnp.int32, (PAIR, PAIR), 0)
    col = lax.broadcasted_iota(jnp.int32, (PAIR, PAIR), 1)
    pairs = e // PAIR
    for t in range(rows // PAIR):
        first = counts[base + 2 * t]
        second = counts[base + 2 * t + 1]
        valid = ((row < VIS) & (col < jnp.minimum(first, VIS))) | (
            (row >= VIS) & (col >= VIS) & (col < VIS + second)
        )
        for p in range(pairs):
            lanes = pl.ds(p * PAIR, PAIR)
            q2 = q_o[rows_of(t), lanes]
            kc = two_heads(k_o[rows_of(t), lanes], low)
            vc = two_heads(v_o[rows_of(t), lanes], low)
            scores = mm(q2, kc, NT) * (HD**-0.5)
            for h in range(2):
                s = jnp.where(valid, scores[:, h * PAIR : (h + 1) * PAIR], NEG)
                ex = jnp.exp(s - jnp.max(s, axis=-1, keepdims=True))
                probs_o[t * pairs + p, :, pl.ds(h * PAIR, PAIR)] = ex / jnp.sum(
                    ex, axis=-1, keepdims=True
                )
            pb = probs_o[t * pairs + p].astype(BF)
            mixed_o[rows_of(t), lanes] = mm(pb, vc).astype(BF)
    proj_o[...] = mm(mixed_o[...], w[:, 3 * e : 4 * e], NT).astype(BF)


def feed_kernel(at, first, n_alias, x, own, other, small, cot, *refs):
    w_up, refs = weights(refs)
    w_dn, refs = weights(refs)
    b_out, gain, bias, b_up = (small.at[:, at[i] : at[i + 1]] for i in (4, 5, 6, 7))
    if not first:
        sums, refs = refs[0], refs[1:]
    mid_o, norm_o, act_o, gu_o, down_o, gn_o, sums_o = refs[n_alias : n_alias + 7]
    down_acc, gn_acc = refs[n_alias + 7 : n_alias + 9]
    rows, d = x.shape
    f = w_up.shape[1]
    up_at, down_at = at[7], at[8]
    for t in range(rows // PAIR):
        r = rows_of(t)
        middle = x[r, :].astype(F32) + (
            (own[r, :].astype(F32) + other[r, :].astype(F32)) + b_out[...]
        )
        mid_o[r, :] = middle
        xhat, _ = norm_stats(middle)
        norm_o[r, :] = (xhat * gain[...] + bias[...]).astype(BF)
    if first:
        sums_o[...] = jnp.zeros_like(sums_o)
    else:
        sums_o[...] = sums[...]
    sums_o[:, down_at : down_at + d] += col_sum(cot[...].astype(F32))
    tile = 256
    for j in range(f // tile):
        c = pl.ds(j * tile, tile)
        u = mm(norm_o[...], w_up[:, c]) + b_up[:, c]
        ga = mm(cot[...], w_dn[:, c])
        cdf = 0.5 * (1.0 + lax.erf(u * (0.5**0.5)))
        pdf = jnp.exp(u * u * -0.5) * 0.3989422804014327
        act_o[:, c] = (u * cdf).astype(BF)
        gu = (ga * (cdf + u * pdf)).astype(BF)
        gu_o[:, c] = gu
        sums_o[:, up_at + j * tile : up_at + (j + 1) * tile] += col_sum(gu.astype(F32))
        gn = mm(gu, w_up[:, c], NT)
        dn = mm(act_o[:, c], w_dn[:, c], NT)
        if j == 0:
            gn_acc[...] = gn
            down_acc[...] = dn
        else:
            gn_acc[...] += gn
            down_acc[...] += dn
    gn_o[...] = gn_acc[...].astype(BF)
    down_o[...] = down_acc[...].astype(BF)


def back_kernel(at, n_alias, middle, own, other, cot, small, q, k, v, probs, x, sums, *refs):
    w, refs = weights(refs)
    gain2 = small.at[:, at[5] : at[6]]
    gp_o, gqkv_o, gn_o, sums_o = refs[n_alias : n_alias + 4]
    gmix = refs[n_alias + 4]
    rows, d = x.shape
    e = q.shape[1]
    sums_o[...] = sums[...]
    g1_at, b1_at, qv_at, out_at, g2_at, b2_at = (at[i] for i in (0, 1, 2, 4, 5, 6))
    for t in range(rows // PAIR):
        r = rows_of(t)
        gn = own[r, :].astype(F32) + other[r, :].astype(F32)
        xhat, inv = norm_stats(middle[r, :])
        tt = gn * gain2[...]
        grad = cot[r, :].astype(F32) + inv * (
            tt
            - jnp.mean(tt, axis=-1, keepdims=True)
            - xhat * jnp.mean(tt * xhat, axis=-1, keepdims=True)
        )
        gp = grad.astype(BF)
        gp_o[r, :] = gp
        sums_o[:, g2_at : g2_at + d] += col_sum(gn * xhat)
        sums_o[:, b2_at : b2_at + d] += col_sum(gn)
        sums_o[:, out_at : out_at + d] += col_sum(gp.astype(F32))
    gmix[...] = mm(gp_o[...], w[:, 3 * e : 4 * e]).astype(BF)
    low = low_lanes((PAIR, PAIR))
    pairs = e // PAIR
    for t in range(rows // PAIR):
        r = rows_of(t)
        for p in range(pairs):
            lanes = pl.ds(p * PAIR, PAIR)
            q2 = q[r, lanes]
            g2 = gmix[r, lanes]
            kc = two_heads(k[r, lanes], low)
            vc = two_heads(v[r, lanes], low)
            pr = probs[t * pairs + p]
            gprob = mm(g2, vc, NT)
            prod = pr * gprob
            tot = jnp.concatenate(
                [
                    jnp.broadcast_to(
                        jnp.sum(prod[:, h * PAIR : (h + 1) * PAIR], axis=-1, keepdims=True),
                        (PAIR, PAIR),
                    )
                    for h in range(2)
                ],
                axis=1,
            )
            gs = (pr * (gprob - tot)).astype(BF)
            gq = mm(gs, kc) * (HD**-0.5)
            gk = mm(gs, q2, TN)
            gv = mm(pr.astype(BF), g2, TN)
            gqkv_o[r, pl.ds(p * PAIR, PAIR)] = gq.astype(BF)
            gqkv_o[r, pl.ds(e + p * PAIR, PAIR)] = (
                jnp.where(low, gk[:PAIR], gk[PAIR:]) * (HD**-0.5)
            ).astype(BF)
            gqkv_o[r, pl.ds(2 * e + p * PAIR, PAIR)] = jnp.where(
                low, gv[:PAIR], gv[PAIR:]
            ).astype(BF)
    sums_o[:, qv_at : qv_at + e] += col_sum(gqkv_o[:, 0:e].astype(F32))
    sums_o[:, qv_at + e : qv_at + 2 * e] += col_sum(gqkv_o[:, 2 * e : 3 * e].astype(F32))
    gn_o[...] = mm(gqkv_o[...], w[:, 0 : 3 * e], NT).astype(BF)
    for t in range(rows // PAIR):
        r = rows_of(t)
        xhat, _ = norm_stats(x[r, :].astype(F32))
        gn = gn_o[r, :].astype(F32)
        sums_o[:, g1_at : g1_at + d] += col_sum(gn * xhat)
        sums_o[:, b1_at : b1_at + d] += col_sum(gn)


def rows_kernel(at, n_alias, x, own, other, gm, small, *refs):
    gain = small.at[:, at[0] : at[1]]
    (out,) = refs[n_alias:]
    for t in range(x.shape[0] // PAIR):
        r = rows_of(t)
        gn = own[r, :].astype(F32) + other[r, :].astype(F32)
        xhat, inv = norm_stats(x[r, :].astype(F32))
        tt = gn * gain[...]
        out[r, :] = (
            gm[r, :].astype(F32)
            + inv
            * (
                tt
                - jnp.mean(tt, axis=-1, keepdims=True)
                - xhat * jnp.mean(tt * xhat, axis=-1, keepdims=True)
            )
        ).astype(BF)


def chunk_spec(shape, ch):
    return pl.BlockSpec(
        shape, lambda i: (ch,) + (0,) * (len(shape) - 1), pipeline_mode=pl.Buffered(1)
    )


def whole_spec(shape):
    return pl.BlockSpec(shape, lambda i: (0,) * len(shape), pipeline_mode=pl.Buffered(1))


SMEM_SPEC = pl.BlockSpec(memory_space=pltpu.SMEM)


def call(kernel, ch, n_ch, inputs, kept, fresh, scratch=(), name=None, deps=(), us=1.0, mib=8):
    in_specs, args = [], []
    for arr, kind in inputs:
        args.append(arr)
        if kind == "s":
            in_specs.append(SMEM_SPEC)
        elif kind == "c":
            in_specs.append(chunk_spec((arr.shape[0] // n_ch,) + arr.shape[1:], ch))
        else:
            in_specs.append(whole_spec(arr.shape))
    out_shapes, out_specs, aliases = [], [], {}
    for i, (shape, dtype, previous) in enumerate(kept):
        out_shapes.append(jax.ShapeDtypeStruct(shape, dtype))
        out_specs.append(chunk_spec((shape[0] // n_ch,) + shape[1:], ch))
        if previous is not None:
            aliases[len(args)] = i
            args.append(previous)
            in_specs.append(pl.BlockSpec(memory_space=pl.ANY))
    args += list(deps)
    in_specs += [pl.BlockSpec(memory_space=pl.ANY)] * len(deps)
    for shape, dtype in fresh:
        out_shapes.append(jax.ShapeDtypeStruct(shape, dtype))
        out_specs.append(whole_spec(shape))
    return pl.pallas_call(
        functools.partial(kernel, len(aliases) + len(deps)),
        grid=(1,),
        in_specs=in_specs,
        out_specs=out_specs,
        out_shape=out_shapes,
        scratch_shapes=list(scratch),
        input_output_aliases=aliases,
        compiler_params=pltpu.CompilerParams(vmem_limit_bytes=mib * MIB),
        cost_estimate=cost(us),
        name=name,
    )(*args)


SCALE = 0.001


def cost(us):
    return pl.CostEstimate(flops=int(us * SCALE * 1.1e9), bytes_accessed=0, transcendentals=0)


def after(x, *deps):
    return lax.optimization_barrier((x,) + deps)[0]


class Links:
    def __init__(self, n):
        self.n = n
        self.depth = n // 4
        me = lax.axis_index("dp")
        self.core, self.x, self.z = me % 2, (me // 2) % 2, me // 4
        self.where = jnp.stack([self.z, self.x, self.core]).astype(jnp.int32)

    def core_swap(self, v):
        return lax.ppermute(v, "dp", [(i, i ^ 1) for i in range(self.n)])

    def x_swap(self, v):
        return lax.ppermute(v, "dp", [(i, i ^ 2) for i in range(self.n)])

    def z_shift(self, v, k):
        return lax.ppermute(v, "dp", [(i, (i + 4 * k) % self.n) for i in range(self.n)])

    def z_xor(self, v, k):
        return lax.ppermute(v, "dp", [(i, i ^ (4 * k)) for i in range(self.n)])


def y_swap(v):
    return lax.ppermute(v, "tensor", [(0, 1), (1, 0)])


def y_chain(parts):
    got = []
    for p in parts:
        got.append(y_swap(after(p, *got[-1:])))
    return got


def simple(kernel, name, us, inputs, outs, deps=(), **kw):
    specs = [SMEM_SPEC if kind == "s" else whole_spec(a.shape) for a, kind in inputs]
    specs += [pl.BlockSpec(memory_space=pl.ANY)] * len(deps)
    n_in = len(inputs)

    def body(*refs):
        kernel(*refs[:n_in], *refs[n_in + len(deps) :], **kw)

    return pl.pallas_call(
        body,
        grid=(1,),
        in_specs=specs,
        out_specs=[whole_spec(shape) for shape, _ in outs],
        out_shape=[jax.ShapeDtypeStruct(shape, dtype) for shape, dtype in outs],
        compiler_params=pltpu.CompilerParams(vmem_limit_bytes=8 * MIB),
        cost_estimate=cost(us),
        name=name,
    )(*[a for a, _ in inputs], *deps)


def stack_kernel(where, *refs):
    out = refs[-1]
    depth = out.shape[0]
    for k in range(depth):
        out[lax.rem(where[0] - k + depth, depth)] = refs[k][...]


def gather_z(links, own):
    return [own] + [links.z_shift(own, k) for k in range(1, links.depth)]


def stack_z(links, parts, deps=()):
    shape = (links.depth,) + parts[0].shape
    inputs = [(links.where, "s")] + [(p, "w") for p in parts]
    return simple(stack_kernel, "stack", 2.0, inputs, [(shape, BF)], deps)[0]


def grad_kernel(where, *refs):
    keep, send = refs[-2:]
    n, r, _ = keep.shape
    tile = 2 * n * r
    pairs = [(refs[i], refs[i + 1]) for i in range(0, len(refs) - 2, 2)]
    at = 0
    for left, right in pairs:
        width = right.shape[1]
        g = mm(left[...], right[...], TN).astype(BF).reshape(n, 2, r, width)
        cols = pl.ds(at, width)
        for c in range(2):

            @pl.when(where[2] == c)
            def _(g=g, c=c, cols=cols):
                keep[:, :, cols] = g[:, c]
                send[:, :, cols] = g[:, 1 - c]

        at += width


def weight_grad(links, name, us, pairs, deps=()):
    rows, d = pairs[0][0].shape
    n, r = links.n // 2, d // links.n
    width = sum(right.shape[1] for _, right in pairs)
    steps = 2
    specs, args = [SMEM_SPEC], [links.where]
    for left, right in pairs:
        specs.append(pl.BlockSpec((rows, d // steps), lambda i: (0, i)))
        specs.append(whole_spec(right.shape))
        args += [left, right]
    n_in = len(args)

    def body(*refs):
        grad_kernel(*refs[:n_in], *refs[n_in + len(deps) :])

    return pl.pallas_call(
        body,
        grid=(steps,),
        in_specs=specs + [pl.BlockSpec(memory_space=pl.ANY)] * len(deps),
        out_specs=[pl.BlockSpec((n // steps, r, width), lambda i: (i, 0, 0))] * 2,
        out_shape=[jax.ShapeDtypeStruct((n, r, width), BF)] * 2,
        compiler_params=pltpu.CompilerParams(vmem_limit_bytes=20 * MIB),
        cost_estimate=cost(us),
        name=name,
    )(*args, *deps)


def add_core_kernel(where, mine, got, keep, send):
    for zz in range(keep.shape[0]):
        a, b = 2 * zz + where[1], 2 * zz + 1 - where[1]
        keep[zz] = mine[a] + got[a]
        send[zz] = mine[b] + got[b]


def add_core(links, mine, got, deps=()):
    shape = (links.depth,) + mine.shape[1:]
    inputs = [(links.where, "s"), (mine, "w"), (got, "w")]
    return simple(add_core_kernel, "add_core", 1.5, inputs, [(shape, BF)] * 2, deps)


def add_x_kernel(where, mine, got, keep, *send):
    depth = mine.shape[0]
    for k in range(depth):
        zz = lax.rem(where[0] + k, depth)
        if k == 0:
            keep[...] = mine[zz].astype(F32) + got[zz].astype(F32)
        else:
            send[k - 1][...] = mine[zz] + got[zz]


def add_x(links, mine, got, deps=()):
    shape = mine.shape[1:]
    inputs = [(links.where, "s"), (mine, "w"), (got, "w")]
    outs = [(shape, F32)] + [(shape, BF)] * (links.depth - 1)
    return simple(add_x_kernel, "add_x", 1.2, inputs, outs, deps)


def send_z(links, parts):
    return [links.z_shift(p, k + 1) for k, p in enumerate(parts)]


def total_z(mine, got):
    for part in got:
        mine = mine + part.astype(F32)
    return mine


def out_kernel(at, n_alias, middle, own, other, small, *refs):
    bias = small.at[:, at[8] : at[9]]
    out = refs[n_alias]
    for t in range(middle.shape[0] // PAIR):
        r = rows_of(t)
        down = own[r, :].astype(F32) + other[r, :].astype(F32)
        out[r, :] = (middle[r, :] + (down + bias[...])).astype(BF)


def split_kernel(at, a, b, *outs):
    total = a[...] + b[...]
    for i, out in enumerate(outs):
        out[...] = total[0, at[i] : at[i + 1]]


def local(
    n_dp,
    patches,
    visible,
    cotangent,
    ln1_gain,
    ln1_bias,
    w_qkv,
    b_qkv,
    w_out,
    b_out,
    ln2_gain,
    ln2_bias,
    w_up,
    b_up,
    w_down,
    b_down,
):
    samples, vis, d = patches.shape
    rows = samples * vis
    e = w_qkv.shape[2]
    f = w_up.shape[1]
    n_ch = 2
    per = rows // n_ch
    fast = n_dp == 16
    links = Links(n_dp)

    at = [0]
    for size in (d, d, e, e, d, d, d, f, d):
        at.append(at[-1] + size)
    n_sums = at[-1]
    small = jnp.concatenate(
        [ln1_gain, ln1_bias, b_qkv[0], b_qkv[1], b_out, ln2_gain, ln2_bias, b_up, b_down]
    ).reshape(1, n_sums)
    x = patches.reshape(rows, d)
    cot = cotangent.reshape(rows, d)
    groups = rows // PAIR * (e // PAIR)

    own_att = jnp.concatenate([w_qkv[0], w_qkv[1], w_qkv[2], w_out.T], axis=1)
    own_dn = w_down.T
    if fast:
        z_att = gather_z(links, own_att)
        a_att = stack_z(links, z_att)
        x_att = links.x_swap(a_att)
        z_up = gather_z(links, after(w_up, *z_att))
        z_dn = gather_z(links, after(own_dn, *z_up))
        w_att = [
            (links.where, "s"),
            (a_att, "w"),
            (x_att, "w"),
            (links.core_swap(a_att), "w"),
            (links.core_swap(after(x_att, *z_up)), "w"),
        ]
        buf = [pltpu.VMEM((d, 4 * e), BF)]
        a_up = stack_z(links, z_up)
        x_up = links.x_swap(a_up)
    else:
        w_att, w_upf, w_dnf = (
            [(lax.all_gather(w, "dp", axis=0, tiled=True), "w")] for w in (own_att, w_up, own_dn)
        )
        buf = []

    y_last = []

    def exchange(v):
        got = y_swap(after(v, *y_last))
        y_last[:] = [got]
        return got

    def attend(ch, kept, deps):
        return call(
            functools.partial(attend_kernel, ch * (samples // n_ch), at),
            ch,
            n_ch,
            [(visible, "s"), (x, "c"), (small, "w")] + w_att,
            [
                ((rows, d), BF, kept[0]),
                ((rows, e), BF, kept[1]),
                ((rows, e), BF, kept[2]),
                ((rows, e), BF, kept[3]),
                ((groups, PAIR, 2 * PAIR), F32, kept[4]),
                ((rows, e), BF, kept[5]),
            ],
            [((per, d), BF)],
            scratch=buf,
            name=f"attend{ch}",
            us=5.4,
            mib=16,
            deps=deps,
        )

    def feed(ch, kept, sums, deps):
        return call(
            functools.partial(feed_kernel, at, ch == 0),
            ch,
            n_ch,
            [(x, "c"), (proj[ch], "w"), (proj_got[ch], "w"), (small, "w"), (cot, "c")]
            + w_upf
            + w_dnf
            + ([] if ch == 0 else [(sums, "w")]),
            [
                ((rows, d), F32, kept[0]),
                ((rows, d), BF, kept[1]),
                ((rows, f), BF, kept[2]),
                ((rows, f), BF, kept[3]),
            ],
            [((per, d), BF), ((per, d), BF), ((1, n_sums), F32)],
            scratch=[pltpu.VMEM((per, d), F32), pltpu.VMEM((per, d), F32)]
            + [pltpu.VMEM((d, f), BF)] * (2 if fast else 0),
            name=f"feed{ch}",
            us=10.2,
            mib=26,
            deps=deps,
        )

    def back(ch, kept, sums, deps):
        return call(
            functools.partial(back_kernel, at),
            ch,
            n_ch,
            [
                (middle, "c"),
                (gn2[ch], "w"),
                (gn2_got[ch], "w"),
                (cot, "c"),
                (small, "w"),
                (q, "c"),
                (k, "c"),
                (v, "c"),
                (probs, "c"),
                (x, "c"),
                (sums, "w"),
            ]
            + w_att,
            [((rows, d), BF, kept[0]), ((rows, 3 * e), BF, kept[1])],
            [((per, d), BF), ((1, n_sums), F32)],
            scratch=[pltpu.VMEM((per, e), BF)] + buf,
            name=f"back{ch}",
            us=9.6,
            mib=20,
            deps=deps,
        )

    proj, proj_got = [None] * n_ch, [None] * n_ch
    *kept, proj[0] = attend(0, [None] * 6, z_up[1:] if fast else ())
    proj_got[0] = exchange(proj[0])
    if fast:
        a_dn = stack_z(links, z_dn, (proj[0],))
        x_dn = links.x_swap(a_dn)
    *kept, proj[1] = attend(1, kept, (x_up, a_dn) if fast else ())
    norm1, q, k, v, probs, mixed = kept
    proj_got[1] = exchange(proj[1])
    if fast:
        w_upf, w_dnf = (
            [
                (links.where, "s"),
                (a, "w"),
                (b, "w"),
                (links.core_swap(after(a, proj[1], proj_got[0])), "w"),
                (links.core_swap(after(b, proj[1], proj_got[0])), "w"),
            ]
            for a, b in ((a_up, x_up), (a_dn, x_dn))
        )

    down, gn2, gn2_got = [None] * n_ch, [None] * n_ch, [None] * n_ch
    *kept, down[0], gn2[0], sums = feed(0, [None] * 4, None, ())
    gn2_got[0] = exchange(gn2[0])
    *kept, down[1], gn2[1], sums = feed(1, kept, sums, ())
    middle, norm2, active, grad_up = kept
    gn2_got[1] = exchange(gn2[1])
    if fast:
        k_dn, s_dn = weight_grad(links, "grad_dn", 3.8, [(cot, active)], (gn2_got[0],))
        k_up, s_up = weight_grad(links, "grad_up", 3.8, [(norm2, grad_up)], (s_dn,))
        c_dn = links.core_swap(s_dn)
        c_up = links.core_swap(s_up)
        k_dn, s_dn = add_core(links, k_dn, c_dn, (k_up,))
        x_dn = links.x_swap(s_dn)

    gn1, gn1_got = [None] * n_ch, [None] * n_ch
    *kept, gn1[0], sums = back(0, [None] * 2, sums, (s_dn, c_up) if fast else ())
    gn1_got[0] = exchange(gn1[0])
    if fast:
        k_up, s_up = add_core(links, k_up, c_up, (gn1[0],))
        x_up = links.x_swap(s_up)
    *kept, gn1[1], sums = back(1, kept, sums, (x_dn, s_up) if fast else ())
    grad_proj, grad_qkv = kept
    gn1_got[1] = exchange(gn1[1])
    down_got = [exchange(a) for a in down]

    if fast:
        k_dn, *s_dn = add_x(links, k_dn, x_dn, (gn1[1],))
        z_dn = send_z(links, s_dn)
        k_att, s_att = weight_grad(
            links, "grad_att", 4.0, [(norm1, grad_qkv), (grad_proj, mixed)], s_dn[-1:]
        )
        c_att = links.core_swap(s_att)
        k_att, s_att = add_core(links, k_att, c_att)
        x_att = links.x_swap(after(s_att, x_up))
        k_up, *s_up = add_x(links, k_up, x_up, (s_att,))
        z_up = send_z(links, [after(a, *z_dn) for a in s_up])
        g_dn = total_z(k_dn, z_dn)
        k_att, *s_att = add_x(links, k_att, x_att)
        z_att = send_z(links, [after(a, *z_up) for a in s_att])
        g_up = total_z(k_up, z_up)
        g_att = total_z(k_att, z_att)
        lane = lax.broadcasted_iota(jnp.int32, sums.shape, 1)
        sums = sums + jnp.where(lane < 2 * d, y_swap(sums), 0.0)
        sums = sums + links.core_swap(sums)
        sums = sums + links.x_swap(sums)
        sums = sums + links.z_xor(sums, 1)
        halves = [sums, links.z_xor(sums, 2)]
    else:
        g_dn, g_up, g_att = (
            lax.psum_scatter(mm(a, b, TN).astype(BF), "dp", scatter_dimension=0, tiled=True)
            for a, b in ((cot, active), (norm2, grad_up), (norm1, grad_qkv))
        )
        g_out = lax.psum_scatter(
            mm(grad_proj, mixed, TN).astype(BF), "dp", scatter_dimension=0, tiled=True
        )
        g_att = jnp.concatenate([g_att, g_out], axis=1)
        g_dn, g_up, g_att = (g.astype(F32) for g in (g_dn, g_up, g_att))
        lane = lax.broadcasted_iota(jnp.int32, sums.shape, 1)
        sums = lax.psum(sums + jnp.where(lane < 2 * d, y_swap(sums), 0.0), "dp")
        halves = [sums, jnp.zeros_like(sums)]

    grad_rows = output = None
    for ch in range(n_ch):
        (grad_rows,) = call(
            functools.partial(rows_kernel, at),
            ch,
            n_ch,
            [(x, "c"), (gn1[ch], "w"), (gn1_got[ch], "w"), (grad_proj, "c"), (small, "w")],
            [((rows, d), BF, grad_rows)],
            [],
            name=f"rows{ch}",
            us=3.5,
            mib=8,
        )
    for ch in range(n_ch):
        (output,) = call(
            functools.partial(out_kernel, at),
            ch,
            n_ch,
            [(middle, "c"), (down[ch], "w"), (down_got[ch], "w"), (small, "w")],
            [((rows, d), BF, output)],
            [],
            name=f"out{ch}",
            us=2.0,
            mib=8,
        )

    cuts = [0, d, 2 * d, 2 * d + 2 * e] + at[5:]
    part = simple(
        functools.partial(split_kernel, cuts),
        "split",
        1.0,
        [(h, "w") for h in halves],
        [((b - a,), F32) for a, b in zip(cuts, cuts[1:])],
    )
    return (
        output.reshape(patches.shape),
        grad_rows.reshape(patches.shape),
        part[0],
        part[1],
        jnp.stack([g_att[:, 0:e], g_att[:, e : 2 * e], g_att[:, 2 * e : 3 * e]]),
        part[2].reshape(2, e),
        g_att[:, 3 * e : 4 * e].T,
        part[3],
        part[4],
        part[5],
        g_up,
        part[6],
        g_dn.T,
        part[7],
    )


def solution(mesh):
    return jax.shard_map(
        functools.partial(local, mesh.shape["dp"]),
        mesh=mesh,
        in_specs=(
            P("dp", None, None),
            P("dp"),
            P("dp", None, None),
            P(),
            P(),
            P(None, "dp", "tensor"),
            P(None, "tensor"),
            P("tensor", "dp"),
            P(),
            P(),
            P(),
            P("dp", "tensor"),
            P("tensor"),
            P("tensor", "dp"),
            P(),
        ),
        out_specs=(
            P("dp", None, None),
            P("dp", None, None),
            P(),
            P(),
            P(None, "dp", "tensor"),
            P(None, "tensor"),
            P("tensor", "dp"),
            P(),
            P(),
            P(),
            P("dp", "tensor"),
            P("tensor"),
            P("tensor", "dp"),
            P(),
        ),
        check_vma=False,
    )
```

```python
import enum
import functools

import jax
import jax.numpy as jnp
from jax import lax
from jax.experimental import pallas as pl
from jax.experimental.pallas import tpu as pltpu
from jax.sharding import PartitionSpec as P

HD = 64
VIS = 64
EPS = 1e-06
BF = jnp.bfloat16
F32 = jnp.float32
NEG = -1000000000.0
PAIR = 2 * VIS
PLACE = 6
X, Y, Z_LOW, Z_HIGH = 1, 3, 4, 5

class K(enum.Enum):
    y_bias = enum.auto()
    z2_att = enum.auto()
    z2_dn = enum.auto()
    z2_up = enum.auto()
    p_att = enum.auto()
    z1_att = enum.auto()
    a_att = enum.auto()
    x_att = enum.auto()
    y_att = enum.auto()
    p_dn = enum.auto()
    z1_dn = enum.auto()
    p_up = enum.auto()
    x_up = enum.auto()
    c_att = enum.auto()
    a_dn = enum.auto()
    x_dn = enum.auto()
    px_up = enum.auto()
    z1_up = enum.auto()
    c_x_att = enum.auto()
    xy_att = enum.auto()
    c_y_att = enum.auto()
    c_xy_att = enum.auto()
    small = enum.auto()
    c_dn1 = enum.auto()
    c_dn2 = enum.auto()
    a_up = enum.auto()
    c_up = enum.auto()
    attend0 = enum.auto()
    feed0 = enum.auto()
    y_gn2_0 = enum.auto()
    attend1 = enum.auto()
    feed1 = enum.auto()
    y_gn2_1 = enum.auto()
    grad_dn = enum.auto()
    gc_dn = enum.auto()
    grad_up = enum.auto()
    gc_up = enum.auto()
    add_c_dn = enum.auto()
    gx_dn = enum.auto()
    add_c_up = enum.auto()
    gx_up = enum.auto()
    back0 = enum.auto()
    add_x_dn = enum.auto()
    gz1_dn = enum.auto()
    back1 = enum.auto()
    grad_qkv = enum.auto()
    gc_qkv = enum.auto()
    add_c_qkv = enum.auto()
    gx_qkv = enum.auto()
    grad_out = enum.auto()
    gc_out = enum.auto()
    rows0 = enum.auto()
    down0 = enum.auto()
    y_down0 = enum.auto()
    add_z_dn = enum.auto()
    gz2_dn = enum.auto()
    rows1 = enum.auto()
    down1 = enum.auto()
    y_down1 = enum.auto()
    c_sums = enum.auto()
    add_x_up = enum.auto()
    gz1_up = enum.auto()
    add_x_qkv = enum.auto()
    gz1_qkv = enum.auto()
    add_c_out = enum.auto()
    gz1_out = enum.auto()
    add_z_out = enum.auto()
    gz2_out = enum.auto()
    add_z_up = enum.auto()
    gz2_up = enum.auto()
    add_z_qkv = enum.auto()
    gz2_qkv = enum.auto()
    add_x_out = enum.auto()
    gx_out = enum.auto()
    finish_dn = enum.auto()
    finish_up = enum.auto()
    finish_out = enum.auto()
    out0 = enum.auto()
    out1 = enum.auto()
    finish_qkv = enum.auto()


MIB = 1024 * 1024
TILE = 256

NN = (((1,), (0,)), ((), ()))
NT = (((1,), (1,)), ((), ()))
TN = (((0,), (0,)), ((), ()))


def mm(left, right, dims=NN):
    return lax.dot_general(left, right, dims, preferred_element_type=F32)


def rows_of(t):
    return pl.ds(t * PAIR, PAIR)


def norm_stats(v):
    mean = jnp.mean(v, axis=-1, keepdims=True)
    centred = v - mean
    inv = lax.rsqrt(jnp.mean(centred * centred, axis=-1, keepdims=True) + EPS)
    return centred * inv, inv


def low_lanes(shape):
    return lax.broadcasted_iota(jnp.int32, shape, 1) < HD


def two_heads(block, low):
    zero = jnp.zeros_like(block)
    return jnp.concatenate([jnp.where(low, block, zero), jnp.where(low, zero, block)], axis=0)


def col_sum(v):
    return jnp.sum(v, axis=0, keepdims=True)


def lay_out(where, parts, buf):
    blocks, r, _ = parts[0].shape
    for b in range(blocks):
        for i, part in enumerate(parts):
            cc = where[2] if i < len(parts) // 2 else 1 - where[2]
            if len(parts) == 2:
                place = b * 2 + cc
            else:
                xx = where[1] if i % 2 == 0 else 1 - where[1]
                place = (b * 2 + xx) * 2 + cc
            buf[pl.ds(pl.multiple_of(place * r, 16), r), :] = part[b]


def attend_kernel(base, at, n_alias, counts, where, x, small, *refs):
    if len(refs[0].shape) == 3 and refs[0].dtype == BF and refs[0].shape[0] == 2:
        w, refs = refs[0], refs[1:]
        outs, (mixed,) = refs[n_alias : n_alias + 8], refs[n_alias + 8 :]
    else:
        parts, refs = refs[:8], refs[8:]
        outs, (w, mixed) = refs[n_alias : n_alias + 8], refs[n_alias + 8 :]
        lay_out(where, parts[:4], w.at[where[3]])
        lay_out(where, parts[4:], w.at[1 - where[3]])
    norm_o, q_o, k_o, v_o, probs_o, mixed_o, mid_o, norm2_o = outs
    g1, b1, b_q, b_v, b_out, g2, b2 = (small.at[:, at[i] : at[i + 1]] for i in range(7))
    rows, d = x.shape
    e = mixed_o.shape[1]
    for t in range(rows // PAIR):
        xhat, _ = norm_stats(x[rows_of(t), :].astype(F32))
        norm_o[rows_of(t), :] = (xhat * g1[...] + b1[...]).astype(BF)
    n = norm_o[...]
    for h in range(2):
        half = slice(h * e, (h + 1) * e)
        q_o[:, half] = (mm(n, w[h, :, 0:e]) + b_q[:, half]).astype(BF)
        k_o[:, half] = mm(n, w[h, :, e : 2 * e]).astype(BF)
        v_o[:, half] = (mm(n, w[h, :, 2 * e : 3 * e]) + b_v[:, half]).astype(BF)
    low = low_lanes((PAIR, PAIR))
    row = lax.broadcasted_iota(jnp.int32, (PAIR, PAIR), 0)
    col = lax.broadcasted_iota(jnp.int32, (PAIR, PAIR), 1)
    pairs = 2 * e // PAIR
    for t in range(rows // PAIR):
        first = counts[base + 2 * t]
        second = counts[base + 2 * t + 1]
        valid = ((row < VIS) & (col < jnp.minimum(first, VIS))) | (
            (row >= VIS) & (col >= VIS) & (col < VIS + second)
        )
        for p in range(pairs):
            lanes = pl.ds(p * PAIR, PAIR)
            q2 = q_o[rows_of(t), lanes]
            kc = two_heads(k_o[rows_of(t), lanes], low)
            vc = two_heads(v_o[rows_of(t), lanes], low)
            scores = mm(q2, kc, NT) * (HD**-0.5)
            for h in range(2):
                s = jnp.where(valid, scores[:, h * PAIR : (h + 1) * PAIR], NEG)
                ex = jnp.exp(s - jnp.max(s, axis=-1, keepdims=True))
                probs_o[t * pairs + p, :, pl.ds(h * PAIR, PAIR)] = ex / jnp.sum(
                    ex, axis=-1, keepdims=True
                )
            pb = probs_o[t * pairs + p].astype(BF)
            mixed[2 * p // pairs, rows_of(t), pl.ds(p % (pairs // 2) * PAIR, PAIR)] = mm(
                pb, vc
            ).astype(BF)
    mixed_o[...] = mixed[where[3]]
    for t in range(rows // PAIR):
        r = rows_of(t)
        proj = mm(mixed[0, r, :], w[0, :, 3 * e : 4 * e], NT)
        proj = proj + mm(mixed[1, r, :], w[1, :, 3 * e : 4 * e], NT)
        middle = x[r, :].astype(F32) + (proj + b_out[...])
        mid_o[r, :] = middle
        xhat, _ = norm_stats(middle)
        norm2_o[r, :] = (xhat * g2[...] + b2[...]).astype(BF)


def feed_kernel(at, up_at, first, n_alias, n2, small, cot, *refs):
    if first and refs[0].shape == (PLACE,):
        parts_up, refs = (refs[0], refs[1:3]), refs[3:]
        parts_dn, refs = (refs[0], refs[1:5]), refs[5:]
        w_up, w_dn = refs[n_alias + 4 : n_alias + 6]
        lay_out(*parts_up, w_up)
        lay_out(*parts_dn, w_dn)
    else:
        w_up, w_dn, *refs = refs
    b_up = small.at[:, up_at : up_at + w_up.shape[1]]
    if not first:
        sums, *refs = refs
    act_o, gu_o, gn_o, sums_o = refs[n_alias : n_alias + 4]
    f = w_up.shape[1]
    if first:
        sums_o[...] = jnp.zeros_like(sums_o)
    else:
        sums_o[...] = sums[...]
    for j in range(f // TILE):
        c = pl.ds(j * TILE, TILE)
        u = mm(n2[...], w_up[:, c]) + b_up[:, c]
        ga = mm(cot[...], w_dn[:, c])
        cdf = 0.5 * (1.0 + lax.erf(u * (0.5**0.5)))
        pdf = jnp.exp(u * u * -0.5) * 0.3989422804014327
        act_o[:, c] = (u * cdf).astype(BF)
        gu = (ga * (cdf + u * pdf)).astype(BF)
        gu_o[:, c] = gu
        lo = at[7] + j * TILE
        sums_o[:, lo : lo + TILE] += col_sum(gu.astype(F32))
    gn_o[...] = mm(gu_o[...], w_up[...], NT).astype(BF)


def down_kernel(n_alias, act, w_dn, *refs):
    refs[n_alias][...] = mm(act[...], w_dn[...], NT).astype(BF)


def norm_back(grad, gain, xhat, inv):
    t = grad * gain
    return inv * (
        t
        - jnp.mean(t, axis=-1, keepdims=True)
        - xhat * jnp.mean(t * xhat, axis=-1, keepdims=True)
    )


def back_kernel(at, gain, n_alias, middle, own, other, cot, small, q, k, v, probs, sums, w, *refs):
    gp_o, gqkv_o, sums_o = refs[n_alias : n_alias + 3]
    (gmix,) = refs[n_alias + 3 :]
    rows, d = cot.shape
    gain2 = small.at[:, gain : gain + d]
    e = gmix.shape[1] // 2
    sums_o[...] = sums[...]
    out_at, g2_at, b2_at = (at[i] for i in (4, 5, 6))
    for t in range(rows // PAIR):
        r = rows_of(t)
        gn = own[r, :].astype(F32) + other[r, :].astype(F32)
        xhat, inv = norm_stats(middle[r, :])
        gp = (cot[r, :].astype(F32) + norm_back(gn, gain2[...], xhat, inv)).astype(BF)
        gp_o[r, :] = gp
        sums_o[:, g2_at : g2_at + d] += col_sum(gn * xhat)
        sums_o[:, b2_at : b2_at + d] += col_sum(gn)
        sums_o[:, out_at : out_at + d] += col_sum(gp.astype(F32))
    for h in range(2):
        gmix[:, h * e : (h + 1) * e] = mm(gp_o[...], w[h, :, 3 * e : 4 * e]).astype(BF)
    low = low_lanes((PAIR, PAIR))
    pairs = 2 * e // PAIR
    for t in range(rows // PAIR):
        r = rows_of(t)
        for p in range(pairs):
            lanes = pl.ds(p * PAIR, PAIR)
            first = 2 * p // pairs * 3 * e + p % (pairs // 2) * PAIR
            q2 = q[r, lanes]
            g2 = gmix[r, lanes]
            kc = two_heads(k[r, lanes], low)
            vc = two_heads(v[r, lanes], low)
            pr = probs[t * pairs + p]
            gprob = mm(g2, vc, NT)
            prod = pr * gprob
            tot = jnp.concatenate(
                [
                    jnp.broadcast_to(
                        jnp.sum(prod[:, i * PAIR : (i + 1) * PAIR], axis=-1, keepdims=True),
                        (PAIR, PAIR),
                    )
                    for i in range(2)
                ],
                axis=1,
            )
            gs = (pr * (gprob - tot)).astype(BF)
            gq = mm(gs, kc) * (HD**-0.5)
            gk = mm(gs, q2, TN)
            gv = mm(pr.astype(BF), g2, TN)
            gqkv_o[r, pl.ds(first, PAIR)] = gq.astype(BF)
            gqkv_o[r, pl.ds(first + e, PAIR)] = (
                jnp.where(low, gk[:PAIR], gk[PAIR:]) * (HD**-0.5)
            ).astype(BF)
            gqkv_o[r, pl.ds(first + 2 * e, PAIR)] = jnp.where(low, gv[:PAIR], gv[PAIR:]).astype(BF)


def rows_kernel(at, gain, n_alias, where, gqkv, w, x, gp, cot, small, sums, *refs):
    rows_o, sums_o = refs[n_alias : n_alias + 2]
    (gn1,) = refs[n_alias + 2 :]
    rows, d = x.shape
    e = gqkv.shape[1] // 6
    gain1 = small.at[:, gain : gain + d]
    sums_o[...] = sums[...]
    g1_at, b1_at, q_at, v_at, down_at = (at[i] for i in (0, 1, 2, 3, 8))
    mine = pl.multiple_of(where[Y] * 3 * e, PAIR)
    sums_o[:, q_at : q_at + e] += col_sum(gqkv[:, pl.ds(mine, e)].astype(F32))
    mine = pl.multiple_of(where[Y] * 3 * e + 2 * e, PAIR)
    sums_o[:, v_at : v_at + e] += col_sum(gqkv[:, pl.ds(mine, e)].astype(F32))
    sums_o[:, down_at : down_at + d] += col_sum(cot[...].astype(F32))
    gn1[...] = mm(gqkv[:, : 3 * e], w[0, :, 0 : 3 * e], NT) + mm(
        gqkv[:, 3 * e :], w[1, :, 0 : 3 * e], NT
    )
    for t in range(rows // PAIR):
        r = rows_of(t)
        xhat, inv = norm_stats(x[r, :].astype(F32))
        gn = gn1[r, :]
        rows_o[r, :] = (gp[r, :].astype(F32) + norm_back(gn, gain1[...], xhat, inv)).astype(BF)
        sums_o[:, g1_at : g1_at + d] += col_sum(gn * xhat)
        sums_o[:, b1_at : b1_at + d] += col_sum(gn)


def chunk_spec(shape, ch):
    return pl.BlockSpec(
        shape, lambda i: (ch,) + (0,) * (len(shape) - 1), pipeline_mode=pl.Buffered(1)
    )


def whole_spec(shape):
    return pl.BlockSpec(shape, lambda i: (0,) * len(shape), pipeline_mode=pl.Buffered(1))


SMEM_SPEC = pl.BlockSpec(memory_space=pltpu.SMEM)


def call(kernel, ch, n_ch, inputs, kept, fresh, scratch=(), name=None, mib=8):
    deps = need(name)
    in_specs, args = [], []
    for arr, kind in inputs:
        args.append(arr)
        if kind == "s":
            in_specs.append(SMEM_SPEC)
        elif kind == "c":
            in_specs.append(chunk_spec((arr.shape[0] // n_ch,) + arr.shape[1:], ch))
        else:
            in_specs.append(whole_spec(arr.shape))
    out_shapes, out_specs, aliases = [], [], {}
    for i, (shape, dtype, previous) in enumerate(kept):
        out_shapes.append(jax.ShapeDtypeStruct(shape, dtype))
        out_specs.append(chunk_spec((shape[0] // n_ch,) + shape[1:], ch))
        if previous is not None:
            aliases[len(args)] = i
            args.append(previous)
            in_specs.append(pl.BlockSpec(memory_space=pl.ANY))
    args += list(deps)
    in_specs += [pl.BlockSpec(memory_space=pl.ANY)] * len(deps)
    for shape, dtype in fresh:
        out_shapes.append(jax.ShapeDtypeStruct(shape, dtype))
        out_specs.append(whole_spec(shape))
    out = pl.pallas_call(
        functools.partial(kernel, len(aliases) + len(deps)),
        grid=(1,),
        in_specs=in_specs,
        out_specs=out_specs,
        out_shape=out_shapes,
        scratch_shapes=list(scratch),
        input_output_aliases=aliases,
        compiler_params=pltpu.CompilerParams(vmem_limit_bytes=mib * MIB),
        cost_estimate=cost(name),
        name=name.name,
    )(*args)
    return made(name, out)


WEIGHT = {
    K.grad_dn: 15,
    K.add_z_out: 2,
    K.xy_att: 15,
    K.back1: 2,
    K.finish_qkv: 40,
    K.back0: 15,
    K.a_up: 15,
    K.feed0: 15,
    K.out1: 40,
    K.add_x_dn: 40,
    K.add_z_dn: 5,
    K.add_x_qkv: 5,
    K.add_z_qkv: 15,
    K.add_c_up: 40,
    K.add_x_out: 2,
    K.add_c_out: 15,
    K.grad_qkv: 2,
}
ORDER = {
    K.gc_up: [K.y_gn2_0, K.c_dn1],
    K.back0: [K.add_c_dn],
    K.a_att: [K.p_up],
    K.z2_dn: [K.y_bias],
    K.z1_up: [K.a_dn],
    K.z2_att: [K.y_bias],
    K.add_c_up: [K.grad_dn],
    K.out0: [K.finish_dn],
    K.gc_dn: [K.y_gn2_0],
    K.xy_att: [K.z2_up],
    K.out1: [K.gz2_dn],
    K.finish_dn: [K.add_z_qkv],
    K.add_c_out: [K.gz1_up],
    K.attend0: [K.c_dn2],
    K.add_x_up: [K.grad_out],
    K.add_z_qkv: [K.add_z_up],
    K.down1: [K.gx_dn],
    K.grad_dn: [K.a_up],
    K.gc_out: [K.back0],
    K.gz2_up: [K.add_z_out],
    K.add_z_dn: [K.y_down0],
}


def cost(name):
    return pl.CostEstimate(
        flops=int(WEIGHT.get(name, 0) * 1.1e9), bytes_accessed=0, transcendentals=0
    )


MADE = {}


def need(name):
    return tuple(MADE[n] for n in ORDER.get(name, ()) if n in MADE)


def made(name, out):
    MADE[name] = out[-1] if isinstance(out, (list, tuple)) else out
    return out


def after(x, *deps):
    return lax.optimization_barrier((x,) + deps)[0] if deps else x


class Links:
    def __init__(self, n):
        self.n = n
        self.depth = n // 4
        me = lax.axis_index("dp")
        self.core, self.x, self.z = me % 2, (me // 2) % 2, me // 4
        self.y = lax.axis_index("tensor")
        self.where = jnp.stack(
            [self.z, self.x, self.core, self.y, self.z % 2, self.z // 2]
        ).astype(jnp.int32)

    def move(self, name, v, axis, pairs):
        return made(name, lax.ppermute(after(v, *need(name)), axis, pairs))

    def core_swap(self, name, v):
        return self.move(name, v, "dp", [(i, i ^ 1) for i in range(self.n)])

    def x_swap(self, name, v):
        return self.move(name, v, "dp", [(i, i ^ 2) for i in range(self.n)])

    def z_low(self, name, v):
        return self.move(name, v, "dp", [(i, i ^ 4) for i in range(self.n)])

    def z_high(self, name, v):
        return self.move(name, v, "dp", [(i, i ^ 8) for i in range(self.n)])

    def y_swap(self, name, v):
        return self.move(name, v, "tensor", [(0, 1), (1, 0)])


def simple(kernel, name, inputs, outs, **kw):
    deps = need(name)
    specs = [SMEM_SPEC if kind == "s" else whole_spec(a.shape) for a, kind in inputs]
    specs += [pl.BlockSpec(memory_space=pl.ANY)] * len(deps)
    n_in = len(inputs)

    def body(*refs):
        kernel(*refs[:n_in], *refs[n_in + len(deps) :], **kw)

    out = pl.pallas_call(
        body,
        grid=(1,),
        in_specs=specs,
        out_specs=[whole_spec(shape) for shape, _ in outs],
        out_shape=[jax.ShapeDtypeStruct(shape, dtype) for shape, dtype in outs],
        compiler_params=pltpu.CompilerParams(vmem_limit_bytes=8 * MIB),
        cost_estimate=cost(name),
        name=name.name,
    )(*[a for a, _ in inputs], *deps)
    return made(name, out)


def small_kernel(where, mine, got, *refs):
    out, row = refs[-1], [a[...].reshape(1, -1) for a in refs[:-1]]
    swap = where[3] == 0
    first, second = mine[...], got[...]
    first, second = jnp.where(swap, first, second), jnp.where(swap, second, first)
    row[2:2] = [first[0:1], second[0:1], first[1:2], second[1:2]]
    at = 0
    for a in row:
        out[:, at : at + a.shape[1]] = a
        at += a.shape[1]


def index_of(i, bit, inner):
    return (i // inner * 2 + bit) * inner + i % inner


def merge_kernel(where, own, got, out, axis, inner):
    bit = where[axis]
    if len(own.shape) == 2:
        out[bit] = own[...]
        out[1 - bit] = got[...]
        return
    for i in range(own.shape[0]):
        out[index_of(i, bit, inner)] = own[i]
        out[index_of(i, 1 - bit, inner)] = got[i]


def merge(links, name, own, got, axis, inner=1):
    shape = (2 * own.size // (own.shape[-1] * own.shape[-2]),) + own.shape[-2:]
    inputs = [(links.where, "s"), (own, "w"), (got, "w")]
    return simple(merge_kernel, name, inputs, [(shape, BF)], axis=axis, inner=inner)[0]


def grad_kernel(where, left, right, keep, send):
    n, r, width = keep.shape
    if right.shape[1] == width:
        g = mm(left[...], right[...], TN)
    else:
        mine = pl.multiple_of(where[Y] * width, PAIR)
        g = mm(left[...], right[:, pl.ds(mine, width)], TN)
    g = g.astype(BF).reshape(n, 2, r, width)
    for c in range(2):

        @pl.when(where[2] == c)
        def _(g=g, c=c):
            keep[...] = g[:, c]
            send[...] = g[:, 1 - c]


def weight_grad(links, name, left, right, width):
    deps = need(name)
    rows, d = left.shape
    n, r = links.n // 2, d // links.n
    steps = 2

    def body(*refs):
        grad_kernel(*refs[:3], *refs[3 + len(deps) :])

    out = pl.pallas_call(
        body,
        grid=(steps,),
        in_specs=[
            SMEM_SPEC,
            pl.BlockSpec((rows, d // steps), lambda i: (0, i)),
            whole_spec(right.shape),
        ]
        + [pl.BlockSpec(memory_space=pl.ANY)] * len(deps),
        out_specs=[pl.BlockSpec((n // steps, r, width), lambda i: (i, 0, 0))] * 2,
        out_shape=[jax.ShapeDtypeStruct((n, r, width), BF)] * 2,
        compiler_params=pltpu.CompilerParams(vmem_limit_bytes=20 * MIB),
        cost_estimate=cost(name),
        name=name.name,
    )(links.where, left, right, *deps)
    return made(name, out)


def halve_kernel(where, mine, got, keep, send, axis):
    bit = where[axis]
    if len(keep.shape) == 2:
        keep[...] = mine[bit].astype(F32) + got[bit].astype(F32)
        send[...] = mine[1 - bit] + got[1 - bit]
        return
    for i in range(keep.shape[0]):
        a, b = 2 * i + bit, 2 * i + 1 - bit
        keep[i] = mine[a] + got[a]
        send[i] = mine[b] + got[b]


def halve(links, name, mine, got, axis):
    n = mine.shape[0] // 2
    shape = mine.shape[1:] if n == 1 else (n,) + mine.shape[1:]
    inputs = [(links.where, "s"), (mine, "w"), (got, "w")]
    outs = [(shape, F32 if n == 1 else BF), (shape, BF)]
    return simple(halve_kernel, name, inputs, outs, axis=axis)


EXTRA = 48


def pack(v, ref, row):
    width = ref.shape[-1]
    ref[row:, :] = jnp.zeros((EXTRA, width), BF)
    for i in range(v.shape[1] // width):
        high = v[:, i * width : (i + 1) * width].astype(BF)
        low = (v[:, i * width : (i + 1) * width] - high.astype(F32)).astype(BF)
        ref[row + i : row + i + 1, :] = high
        ref[row + EXTRA // 2 + i : row + EXTRA // 2 + i + 1, :] = low


def unpack(ref, row, n):
    half = EXTRA // 2
    v = ref[row : row + half, :].astype(F32) + ref[row + half :, :].astype(F32)
    return jnp.concatenate([v[i : i + 1, :] for i in range(n)], axis=1)


def rounded(v):
    high = v.astype(BF).astype(F32)
    return high + (v - high).astype(BF).astype(F32)


def add_core_out_kernel(where, mine, got, sums, sums_got, keep, send, total):
    depth, r, _ = keep.shape
    v = sums[...] + sums_got[...]
    total[...] = rounded(v)
    for i in range(depth):
        a, b = index_of(i, where[Z_LOW], 2), index_of(i, 1 - where[Z_LOW], 2)
        keep[i] = mine[a] + got[a]
        send[i * r : (i + 1) * r, :] = mine[b] + got[b]
    pack(v, send, depth * r)


def add_core_out(links, mine, got, sums, sums_got):
    _, r, e = mine.shape
    inputs = [(links.where, "s")] + [(a, "w") for a in (mine, got, sums, sums_got)]
    outs = [((links.depth, r, e), BF), ((links.depth * r + EXTRA, e), BF), (sums.shape, F32)]
    return simple(add_core_out_kernel, K.add_c_out, inputs, outs)


def halve_sums_kernel(where, mine, got, sums, keep, send, total, axis, inner):
    bit = where[axis]
    n, r, e = mine.shape
    v = sums[...] + unpack(got, n * r, sums.shape[1] // e)
    total[...] = rounded(v)
    for i in range(n // 2):
        a, b = index_of(i, bit, inner), index_of(i, 1 - bit, inner)
        keep[i] = mine[a] + got[pl.ds(pl.multiple_of(a * r, 16), r), :]
        send[i * r : (i + 1) * r, :] = mine[b] + got[pl.ds(pl.multiple_of(b * r, 16), r), :]
    pack(v, send, n // 2 * r)


def halve_sums(links, name, mine, got, sums, axis, inner):
    n, r, e = mine.shape
    inputs = [(links.where, "s"), (mine, "w"), (got, "w"), (sums, "w")]
    outs = [((n // 2, r, e), BF), ((n // 2 * r + EXTRA, e), BF), (sums.shape, F32)]
    return simple(halve_sums_kernel, name, inputs, outs, axis=axis, inner=inner)


def finish_out_kernel(mine, got, sums, g_out, *outs, cuts, pair):
    _, r, e = mine.shape
    g_out[...] = mine[0].astype(F32) + got[0:r, :].astype(F32)
    v = sums[...] + unpack(got, r, sums.shape[1] // e)
    for i, out in enumerate(outs):
        a, b = cuts[i], cuts[i + 1]
        if i == pair:
            out[0:1, :] = v[:, a : (a + b) // 2]
            out[1:2, :] = v[:, (a + b) // 2 : b]
        else:
            out[...] = v[0, a:b]


def finish_out(links, mine, got, sums, cuts, pair):
    _, r, e = mine.shape
    sizes = [(b - a,) for a, b in zip(cuts, cuts[1:])]
    sizes[pair] = (2, sizes[pair][0] // 2)
    outs = [((r, e), F32)] + [(size, F32) for size in sizes]
    inputs = [(a, "w") for a in (mine, got, sums)]
    return simple(finish_out_kernel, K.finish_out, inputs, outs, cuts=cuts, pair=pair)


def finish_kernel(mine, got, out):
    total = mine[...] + got[...].astype(F32)
    if len(out.shape) == 3:
        e = out.shape[2]
        for t in range(3):
            out[t] = total[:, t * e : (t + 1) * e]
    else:
        out[...] = total


def finish(name, mine, got, shape):
    return simple(finish_kernel, name, [(mine, "w"), (got, "w")], [(shape, F32)])[0]


def out_kernel(bias_at, n_alias, middle, own, other, small, *refs):
    bias = small.at[:, bias_at : bias_at + middle.shape[1]]
    out = refs[n_alias]
    for t in range(middle.shape[0] // PAIR):
        r = rows_of(t)
        down = own[r, :].astype(F32) + other[r, :].astype(F32)
        out[r, :] = (middle[r, :] + (down + bias[...])).astype(BF)


def local(
    n_dp,
    patches,
    visible,
    cotangent,
    ln1_gain,
    ln1_bias,
    w_qkv,
    b_qkv,
    w_out,
    b_out,
    ln2_gain,
    ln2_bias,
    w_up,
    b_up,
    w_down,
    b_down,
):
    MADE.clear()
    samples, vis, d = patches.shape
    rows = samples * vis
    e = w_qkv.shape[2]
    f = w_up.shape[1]
    n_ch = 2
    per = rows // n_ch
    fast = n_dp == 16
    links = Links(n_dp)

    at = [0]
    for size in (d, d, e, e, d, d, d, f, d):
        at.append(at[-1] + size)
    n_sums = -(-at[-1] // e) * e
    cuts = [0, d, 2 * d, 2 * d + 2 * e] + at[5:]
    s_at = [0]
    for size in (d, d, 2 * e, 2 * e, d, d, d, f, d):
        s_at.append(s_at[-1] + size)
    b_got = links.y_swap(K.y_bias, b_qkv)
    small = simple(
        small_kernel,
        K.small,
        [(links.where, "s")]
        + [
            (a, "w")
            for a in (b_qkv, b_got, ln1_gain, ln1_bias, b_out, ln2_gain, ln2_bias, b_up, b_down)
        ],
        [((1, s_at[-1]), F32)],
    )[0]
    x = patches.reshape(rows, d)
    cot = cotangent.reshape(rows, d)
    groups = rows // PAIR * (2 * e // PAIR)

    own_att = jnp.concatenate([w_qkv[0], w_qkv[1], w_qkv[2], w_out.T], axis=1)
    own_dn = w_down.T
    if fast:
        z_att = links.z_high(K.z2_att, own_att)
        z_dn = links.z_high(K.z2_dn, own_dn)
        z_up = links.z_high(K.z2_up, w_up)
        p_att = merge(links, K.p_att, own_att, z_att, Z_HIGH)
        a_att = merge(links, K.a_att, p_att, links.z_low(K.z1_att, p_att), Z_LOW)
        x_att = links.x_swap(K.x_att, a_att)
        y_att = links.y_swap(K.y_att, a_att)
        p_dn = merge(links, K.p_dn, own_dn, z_dn, Z_HIGH)
        z_dn = links.z_low(K.z1_dn, p_dn)
        p_up = merge(links, K.p_up, w_up, z_up, Z_HIGH)
        x_up = links.x_swap(K.x_up, p_up)
        c_a = links.core_swap(K.c_att, a_att)
        a_dn = merge(links, K.a_dn, p_dn, z_dn, Z_LOW)
        x_dn = links.x_swap(K.x_dn, a_dn)
        p_up = merge(links, K.px_up, p_up, x_up, X)
        z_up = links.z_low(K.z1_up, p_up)
        c_x = links.core_swap(K.c_x_att, x_att)
        xy_att = links.y_swap(K.xy_att, x_att)
        c_y = links.core_swap(K.c_y_att, y_att)
        c_xy = links.core_swap(K.c_xy_att, xy_att)
        w_att = [(a, "w") for a in (a_att, x_att, c_a, c_x, y_att, xy_att, c_y, c_xy)]
    else:
        w_att, w_upf, w_dnf = (
            lax.all_gather(w, "dp", axis=0, tiled=True) for w in (own_att, w_up, own_dn)
        )
        w_att = [(lax.all_gather(w_att, "tensor", axis=0), "w")]
        w_feed = [(w_upf, "w"), (w_dnf, "w")]

    def attend(ch, kept, w_att):
        lays = len(w_att) > 1
        return call(
            functools.partial(attend_kernel, ch * (samples // n_ch), s_at),
            ch,
            n_ch,
            [(visible, "s"), (links.where, "s"), (x, "c"), (small, "w")] + w_att,
            [
                ((rows, d), BF, kept[0]),
                ((rows, 2 * e), BF, kept[1]),
                ((rows, 2 * e), BF, kept[2]),
                ((rows, 2 * e), BF, kept[3]),
                ((groups, PAIR, 2 * PAIR), F32, kept[4]),
                ((rows, e), BF, kept[5]),
                ((rows, d), F32, kept[6]),
                ((rows, d), BF, kept[7]),
            ],
            [((2, d, 4 * e), BF)] if lays else [],
            scratch=[pltpu.VMEM((2, per, e), BF)],
            name=(K.attend0, K.attend1)[ch],
            mib=20,
        )

    def feed(ch, kept, sums, n2, w_feed):
        lays = len(w_feed) > 2
        return call(
            functools.partial(feed_kernel, at, s_at[7], ch == 0),
            ch,
            n_ch,
            [(n2, "c"), (small, "w"), (cot, "c")] + w_feed + ([] if ch == 0 else [(sums, "w")]),
            [((rows, f), BF, kept[0]), ((rows, f), BF, kept[1])],
            [((per, d), BF), ((1, n_sums), F32)] + ([((d, f), BF)] * 2 if lays else []),
            name=(K.feed0, K.feed1)[ch],
            mib=20,
        )

    def back(ch, kept, sums):
        return call(
            functools.partial(back_kernel, at, s_at[5]),
            ch,
            n_ch,
            [
                (middle, "c"),
                (gn2[ch], "w"),
                (gn2_got[ch], "w"),
                (cot, "c"),
                (small, "w"),
                (q, "c"),
                (k, "c"),
                (v, "c"),
                (probs, "c"),
                (sums, "w"),
                (w_both, "w"),
            ],
            [((rows, d), BF, kept[0]), ((rows, 6 * e), BF, kept[1])],
            [((1, n_sums), F32)],
            scratch=[pltpu.VMEM((per, 2 * e), BF)],
            name=(K.back0, K.back1)[ch],
            mib=20,
        )

    def to_rows(ch, kept, sums):
        return call(
            functools.partial(rows_kernel, at, s_at[0]),
            ch,
            n_ch,
            [
                (links.where, "s"),
                (grad_qkv, "c"),
                (w_both, "w"),
                (x, "c"),
                (grad_proj, "c"),
                (cot, "c"),
                (small, "w"),
                (sums, "w"),
            ],
            [((rows, d), BF, kept)],
            [((1, n_sums), F32)],
            scratch=[pltpu.VMEM((per, d), F32)],
            name=(K.rows0, K.rows1)[ch],
            mib=16,
        )

    if fast:
        c_dn = [links.core_swap(K.c_dn1, a_dn), links.core_swap(K.c_dn2, x_dn)]
        a_up = merge(links, K.a_up, p_up, z_up, Z_LOW, 2)
        w_feed = [(links.where, "s"), (a_up, "w"), (links.core_swap(K.c_up, a_up), "w")]
        w_feed += [(links.where, "s")] + [(a, "w") for a in (a_dn, x_dn, *c_dn)]
    held, kept, sums = [None] * 8, [None] * 2, None
    gn2, gn2_got = [None] * n_ch, [None] * n_ch
    for ch in range(n_ch):
        held = attend(ch, held, w_att)
        if fast and ch == 0:
            *held, w_both = held
            w_att = [(w_both, "w")]
        *kept, gn2[ch], sums, a, b = list(
            feed(ch, kept, sums, held[7], w_feed)
        ) + [None] * (0 if fast and ch == 0 else 2)
        if fast and ch == 0:
            w_feed = [(a, "w"), (b, "w")]
        gn2_got[ch] = links.y_swap((K.y_gn2_0, K.y_gn2_1)[ch], gn2[ch])
    w_both = w_att[0][0]
    norm1, q, k, v, probs, mixed, middle, norm2 = held
    active, grad_up = kept
    if fast:
        k_dn, s_dn = weight_grad(links, K.grad_dn, cot, active, f)
        c_dn = links.core_swap(K.gc_dn, s_dn)
        k_up, s_up = weight_grad(links, K.grad_up, norm2, grad_up, f)
        c_up = links.core_swap(K.gc_up, s_up)
        k_dn, s_dn = halve(links, K.add_c_dn, k_dn, c_dn, X)
        x_dn = links.x_swap(K.gx_dn, s_dn)
        k_up, s_up = halve(links, K.add_c_up, k_up, c_up, X)
        x_up = links.x_swap(K.gx_up, s_up)

    kept = [None] * 2
    for ch in range(n_ch):
        *kept, sums = back(ch, kept, sums)
        if fast and ch == 0:
            k_dn, s_dn = halve(links, K.add_x_dn, k_dn, x_dn, Z_LOW)
            z_dn = links.z_low(K.gz1_dn, s_dn)
    grad_proj, grad_qkv = kept
    if fast:
        k_qkv, s_qkv = weight_grad(links, K.grad_qkv, norm1, grad_qkv, 3 * e)
        c_qkv = links.core_swap(K.gc_qkv, s_qkv)
    if fast:
        k_qkv, s_qkv = halve(links, K.add_c_qkv, k_qkv, c_qkv, X)
        x_qkv = links.x_swap(K.gx_qkv, s_qkv)
        k_out, s_out = weight_grad(links, K.grad_out, grad_proj, mixed, e)
        c_out = links.core_swap(K.gc_out, s_out)
    grad_rows = None
    down, down_got = [None] * n_ch, [None] * n_ch
    for ch in range(n_ch):
        grad_rows, sums = to_rows(ch, grad_rows, sums)
        (down[ch],) = call(
            down_kernel,
            ch,
            n_ch,
            [(active, "c"), w_feed[1]],
            [],
            [((per, d), BF)],
            name=(K.down0, K.down1)[ch],
            mib=10,
        )
        down_got[ch] = links.y_swap((K.y_down0, K.y_down1)[ch], down[ch])
        if fast and ch == 0:
            k_dn, s_dn = halve(links, K.add_z_dn, k_dn, z_dn, Z_HIGH)
            z_dn = links.z_high(K.gz2_dn, s_dn)

    if fast:
        c_sums = links.core_swap(K.c_sums, sums)
        k_up, s_up = halve(links, K.add_x_up, k_up, x_up, Z_LOW)
        z_up = links.z_low(K.gz1_up, s_up)
        k_qkv, s_qkv = halve(links, K.add_x_qkv, k_qkv, x_qkv, Z_LOW)
        z_qkv = links.z_low(K.gz1_qkv, s_qkv)
        k_out, s_out, sums = add_core_out(links, k_out, c_out, sums, c_sums)
        z_out = links.z_low(K.gz1_out, s_out)
        k_out, s_out, sums = halve_sums(links, K.add_z_out, k_out, z_out, sums, Z_HIGH, 2)
        z_out = links.z_high(K.gz2_out, s_out)
        k_up, s_up = halve(links, K.add_z_up, k_up, z_up, Z_HIGH)
        z_up = links.z_high(K.gz2_up, s_up)
        k_qkv, s_qkv = halve(links, K.add_z_qkv, k_qkv, z_qkv, Z_HIGH)
        z_qkv = links.z_high(K.gz2_qkv, s_qkv)
        k_out, s_out, sums = halve_sums(links, K.add_x_out, k_out, z_out, sums, X, 1)
        x_out = links.x_swap(K.gx_out, s_out)
        g_dn = finish(K.finish_dn, k_dn, z_dn, k_dn.shape)
        g_up = finish(K.finish_up, k_up, z_up, k_up.shape)
        g_out, *part = finish_out(links, k_out, x_out, sums, cuts, 2)
    else:
        g_dn, g_up, g_qkv, g_out = (
            lax.psum_scatter(mm(a, b, TN).astype(BF), "dp", scatter_dimension=0, tiled=True)
            for a, b in (
                (cot, active),
                (norm2, grad_up),
                (norm1, lax.dynamic_slice_in_dim(grad_qkv, links.y * 3 * e, 3 * e, axis=1)),
                (grad_proj, mixed),
            )
        )
        g_dn, g_up, g_qkv, g_out = (g.astype(F32) for g in (g_dn, g_up, g_qkv, g_out))
        g_qkv = jnp.stack([g_qkv[:, 0:e], g_qkv[:, e : 2 * e], g_qkv[:, 2 * e : 3 * e]])
        sums = lax.psum(sums, "dp")
        part = [sums[0, a:b] for a, b in zip(cuts, cuts[1:])]
        part[2] = part[2].reshape(2, e)

    output = None
    for ch in range(n_ch):
        (output,) = call(
            functools.partial(out_kernel, s_at[8]),
            ch,
            n_ch,
            [(middle, "c"), (down[ch], "w"), (down_got[ch], "w"), (small, "w")],
            [((rows, d), BF, output)],
            [],
            name=(K.out0, K.out1)[ch],
        )
    if fast:
        g_qkv = finish(K.finish_qkv, k_qkv, z_qkv, (3, k_qkv.shape[0], e))

    return (
        output.reshape(patches.shape),
        grad_rows.reshape(patches.shape),
        part[0],
        part[1],
        g_qkv,
        part[2],
        g_out.T,
        part[3],
        part[4],
        part[5],
        g_up,
        part[6],
        g_dn.T,
        part[7],
    )


def solution(mesh):
    return jax.shard_map(
        functools.partial(local, mesh.shape["dp"]),
        mesh=mesh,
        in_specs=(
            P("dp", None, None),
            P("dp"),
            P("dp", None, None),
            P(),
            P(),
            P(None, "dp", "tensor"),
            P(None, "tensor"),
            P("tensor", "dp"),
            P(),
            P(),
            P(),
            P("dp", "tensor"),
            P("tensor"),
            P("tensor", "dp"),
            P(),
        ),
        out_specs=(
            P("dp", None, None),
            P("dp", None, None),
            P(),
            P(),
            P(None, "dp", "tensor"),
            P(None, "tensor"),
            P("tensor", "dp"),
            P(),
            P(),
            P(),
            P("dp", "tensor"),
            P("tensor"),
            P("tensor", "dp"),
            P(),
        ),
        check_vma=False,
    )
```

```python
import enum
import functools

import jax
import jax.numpy as jnp
from jax import lax
from jax.experimental import pallas as pl
from jax.experimental.pallas import tpu as pltpu
from jax.sharding import PartitionSpec as P

HD = 64
VIS = 64
EPS = 1e-06
BF = jnp.bfloat16
F32 = jnp.float32
NEG = -1000000000.0
PAIR = 2 * VIS
PLACE = 6
X, Y, Z_LOW, Z_HIGH = 1, 3, 4, 5

class K(enum.Enum):
    y_bias = enum.auto()
    z2_att = enum.auto()
    z2_dn = enum.auto()
    z2_up = enum.auto()
    p_att = enum.auto()
    z1_att = enum.auto()
    a_att = enum.auto()
    x_att = enum.auto()
    y_att = enum.auto()
    p_dn = enum.auto()
    z1_dn = enum.auto()
    p_up = enum.auto()
    x_up = enum.auto()
    c_att = enum.auto()
    a_dn = enum.auto()
    x_dn = enum.auto()
    px_up = enum.auto()
    z1_up = enum.auto()
    c_x_att = enum.auto()
    xy_att = enum.auto()
    c_y_att = enum.auto()
    c_xy_att = enum.auto()
    small = enum.auto()
    c_dn1 = enum.auto()
    c_dn2 = enum.auto()
    a_up = enum.auto()
    c_up = enum.auto()
    attend0 = enum.auto()
    feed0 = enum.auto()
    y_gn2_0 = enum.auto()
    attend1 = enum.auto()
    feed1 = enum.auto()
    y_gn2_1 = enum.auto()
    grad_dn = enum.auto()
    gc_dn = enum.auto()
    grad_up = enum.auto()
    gc_up = enum.auto()
    add_c_dn = enum.auto()
    gx_dn = enum.auto()
    add_c_up = enum.auto()
    gx_up = enum.auto()
    back0 = enum.auto()
    add_x_dn = enum.auto()
    gz1_dn = enum.auto()
    back1 = enum.auto()
    grad_qkv = enum.auto()
    gc_qkv = enum.auto()
    add_c_qkv = enum.auto()
    gx_qkv = enum.auto()
    grad_out = enum.auto()
    gc_out = enum.auto()
    rows0 = enum.auto()
    down0 = enum.auto()
    y_down0 = enum.auto()
    add_z_dn = enum.auto()
    gz2_dn = enum.auto()
    rows1 = enum.auto()
    down1 = enum.auto()
    y_down1 = enum.auto()
    c_sums = enum.auto()
    add_x_up = enum.auto()
    gz1_up = enum.auto()
    add_x_qkv = enum.auto()
    gz1_qkv = enum.auto()
    add_c_out = enum.auto()
    gz1_out = enum.auto()
    add_z_out = enum.auto()
    gz2_out = enum.auto()
    add_z_up = enum.auto()
    gz2_up = enum.auto()
    add_z_qkv = enum.auto()
    gz2_qkv = enum.auto()
    add_x_out = enum.auto()
    gx_out = enum.auto()
    finish_dn = enum.auto()
    finish_up = enum.auto()
    finish_out = enum.auto()
    out0 = enum.auto()
    out1 = enum.auto()
    finish_qkv = enum.auto()


MIB = 1024 * 1024
TILE = 256

NN = (((1,), (0,)), ((), ()))
NT = (((1,), (1,)), ((), ()))
TN = (((0,), (0,)), ((), ()))


def mm(left, right, dims=NN):
    return lax.dot_general(left, right, dims, preferred_element_type=F32)


def rows_of(t):
    return pl.ds(t * PAIR, PAIR)


def tile_rows(t):
    return pl.ds(pl.multiple_of(t * PAIR, PAIR), PAIR)


def norm_stats(v):
    mean = jnp.mean(v, axis=-1, keepdims=True)
    centred = v - mean
    inv = lax.rsqrt(jnp.mean(centred * centred, axis=-1, keepdims=True) + EPS)
    return centred * inv, inv


def low_lanes(shape):
    return lax.broadcasted_iota(jnp.int32, shape, 1) < HD


def two_heads(block, low):
    zero = jnp.zeros_like(block)
    return jnp.concatenate([jnp.where(low, block, zero), jnp.where(low, zero, block)], axis=0)


def col_sum(v):
    return jnp.sum(v, axis=0, keepdims=True)


def lay_out(where, parts, buf):
    blocks, r, _ = parts[0].shape
    for b in range(blocks):
        for i, part in enumerate(parts):
            cc = where[2] if i < len(parts) // 2 else 1 - where[2]
            if len(parts) == 2:
                place = b * 2 + cc
            else:
                xx = where[1] if i % 2 == 0 else 1 - where[1]
                place = (b * 2 + xx) * 2 + cc
            buf[pl.ds(pl.multiple_of(place * r, 16), r), :] = part[b]


def attend_kernel(base, at, n_alias, counts, where, x, small, *refs):
    if len(refs[0].shape) == 3 and refs[0].dtype == BF and refs[0].shape[0] == 2:
        w, refs = refs[0], refs[1:]
        outs, (mixed,) = refs[n_alias : n_alias + 8], refs[n_alias + 8 :]
    else:
        parts, refs = refs[:8], refs[8:]
        outs, (w, mixed) = refs[n_alias : n_alias + 8], refs[n_alias + 8 :]
        lay_out(where, parts[:4], w.at[where[3]])
        lay_out(where, parts[4:], w.at[1 - where[3]])
    norm_o, q_o, k_o, v_o, probs_o, mixed_o, mid_o, norm2_o = outs
    g1, b1, b_q, b_v, b_out, g2, b2 = (small.at[:, at[i] : at[i + 1]] for i in range(7))
    rows, d = x.shape
    e = mixed_o.shape[1]
    for t in range(rows // PAIR):
        xhat, _ = norm_stats(x[rows_of(t), :].astype(F32))
        norm_o[rows_of(t), :] = (xhat * g1[...] + b1[...]).astype(BF)
    n = norm_o[...]
    for h in range(2):
        half = slice(h * e, (h + 1) * e)
        q_o[:, half] = (mm(n, w[h, :, 0:e]) + b_q[:, half]).astype(BF)
        k_o[:, half] = mm(n, w[h, :, e : 2 * e]).astype(BF)
        v_o[:, half] = (mm(n, w[h, :, 2 * e : 3 * e]) + b_v[:, half]).astype(BF)
    low = low_lanes((PAIR, PAIR))
    row = lax.broadcasted_iota(jnp.int32, (PAIR, PAIR), 0)
    col = lax.broadcasted_iota(jnp.int32, (PAIR, PAIR), 1)
    pairs = 2 * e // PAIR
    for t in range(rows // PAIR):
        first = counts[base + 2 * t]
        second = counts[base + 2 * t + 1]
        valid = ((row < VIS) & (col < jnp.minimum(first, VIS))) | (
            (row >= VIS) & (col >= VIS) & (col < VIS + second)
        )
        for p in range(pairs):
            lanes = pl.ds(p * PAIR, PAIR)
            q2 = q_o[rows_of(t), lanes]
            kc = two_heads(k_o[rows_of(t), lanes], low)
            vc = two_heads(v_o[rows_of(t), lanes], low)
            scores = mm(q2, kc, NT) * (HD**-0.5)
            for h in range(2):
                s = jnp.where(valid, scores[:, h * PAIR : (h + 1) * PAIR], NEG)
                ex = jnp.exp(s - jnp.max(s, axis=-1, keepdims=True))
                probs_o[t * pairs + p, :, pl.ds(h * PAIR, PAIR)] = ex / jnp.sum(
                    ex, axis=-1, keepdims=True
                )
            pb = probs_o[t * pairs + p].astype(BF)
            mixed[2 * p // pairs, rows_of(t), pl.ds(p % (pairs // 2) * PAIR, PAIR)] = mm(
                pb, vc
            ).astype(BF)
    mixed_o[...] = mixed[where[3]]
    for t in range(rows // PAIR):
        r = rows_of(t)
        proj = mm(mixed[0, r, :], w[0, :, 3 * e : 4 * e], NT)
        proj = proj + mm(mixed[1, r, :], w[1, :, 3 * e : 4 * e], NT)
        middle = x[r, :].astype(F32) + (proj + b_out[...])
        mid_o[r, :] = middle
        xhat, _ = norm_stats(middle)
        norm2_o[r, :] = (xhat * g2[...] + b2[...]).astype(BF)


def feed_kernel(at, up_at, first, n_alias, n2, small, cot, *refs):
    if first and refs[0].shape == (PLACE,):
        parts_up, refs = (refs[0], refs[1:3]), refs[3:]
        parts_dn, refs = (refs[0], refs[1:5]), refs[5:]
        w_up, w_dn = refs[n_alias + 4 : n_alias + 6]
        lay_out(*parts_up, w_up)
        lay_out(*parts_dn, w_dn)
    else:
        w_up, w_dn, *refs = refs
    b_up = small.at[:, up_at : up_at + w_up.shape[1]]
    if not first:
        sums, *refs = refs
    act_o, gu_o, gn_o, sums_o = refs[n_alias : n_alias + 4]
    f = w_up.shape[1]
    if first:
        sums_o[...] = jnp.zeros_like(sums_o)
    else:
        sums_o[...] = sums[...]
    for j in range(f // TILE):
        c = pl.ds(j * TILE, TILE)
        u = mm(n2[...], w_up[:, c]) + b_up[:, c]
        ga = mm(cot[...], w_dn[:, c])
        cdf = 0.5 * (1.0 + lax.erf(u * (0.5**0.5)))
        pdf = jnp.exp(u * u * -0.5) * 0.3989422804014327
        act_o[:, c] = (u * cdf).astype(BF)
        gu = (ga * (cdf + u * pdf)).astype(BF)
        gu_o[:, c] = gu
        lo = at[7] + j * TILE
        sums_o[:, lo : lo + TILE] += col_sum(gu.astype(F32))
    gn_o[...] = mm(gu_o[...], w_up[...], NT).astype(BF)


def down_kernel(n_alias, act, w_dn, *refs):
    refs[n_alias][...] = mm(act[...], w_dn[...], NT).astype(BF)


def norm_back(grad, gain, xhat, inv):
    t = grad * gain
    return inv * (
        t
        - jnp.mean(t, axis=-1, keepdims=True)
        - xhat * jnp.mean(t * xhat, axis=-1, keepdims=True)
    )


def back_kernel(at, gain, n_alias, middle, own, other, cot, small, q, k, v, probs, sums, w, *refs):
    gp_o, gqkv_o, sums_o = refs[n_alias : n_alias + 3]
    (gmix,) = refs[n_alias + 3 :]
    rows, d = cot.shape
    gain2 = small.at[:, gain : gain + d]
    e = gmix.shape[1] // 2
    sums_o[...] = sums[...]
    out_at, g2_at, b2_at = (at[i] for i in (4, 5, 6))
    for t in range(rows // PAIR):
        r = rows_of(t)
        gn = own[r, :].astype(F32) + other[r, :].astype(F32)
        xhat, inv = norm_stats(middle[r, :])
        gp = (cot[r, :].astype(F32) + norm_back(gn, gain2[...], xhat, inv)).astype(BF)
        gp_o[r, :] = gp
        sums_o[:, g2_at : g2_at + d] += col_sum(gn * xhat)
        sums_o[:, b2_at : b2_at + d] += col_sum(gn)
        sums_o[:, out_at : out_at + d] += col_sum(gp.astype(F32))
    for h in range(2):
        gmix[:, h * e : (h + 1) * e] = mm(gp_o[...], w[h, :, 3 * e : 4 * e]).astype(BF)
    low = low_lanes((PAIR, PAIR))
    pairs = 2 * e // PAIR

    @pl.loop(0, rows // PAIR)
    def _(t):
        r = tile_rows(t)
        for p in range(pairs):
            lanes = pl.ds(p * PAIR, PAIR)
            first = 2 * p // pairs * 3 * e + p % (pairs // 2) * PAIR
            q2 = q[r, lanes]
            g2 = gmix[r, lanes]
            kc = two_heads(k[r, lanes], low)
            vc = two_heads(v[r, lanes], low)
            pr = probs[t * pairs + p]
            gprob = mm(g2, vc, NT)
            prod = pr * gprob
            tot = jnp.concatenate(
                [
                    jnp.broadcast_to(
                        jnp.sum(prod[:, i * PAIR : (i + 1) * PAIR], axis=-1, keepdims=True),
                        (PAIR, PAIR),
                    )
                    for i in range(2)
                ],
                axis=1,
            )
            gs = (pr * (gprob - tot)).astype(BF)
            gq = mm(gs, kc) * (HD**-0.5)
            gk = mm(gs, q2, TN)
            gv = mm(pr.astype(BF), g2, TN)
            gqkv_o[r, pl.ds(first, PAIR)] = gq.astype(BF)
            gqkv_o[r, pl.ds(first + e, PAIR)] = (
                jnp.where(low, gk[:PAIR], gk[PAIR:]) * (HD**-0.5)
            ).astype(BF)
            gqkv_o[r, pl.ds(first + 2 * e, PAIR)] = jnp.where(low, gv[:PAIR], gv[PAIR:]).astype(BF)


def rows_kernel(at, gain, n_alias, where, gqkv, w, x, gp, cot, small, sums, *refs):
    rows_o, sums_o = refs[n_alias : n_alias + 2]
    (gn1,) = refs[n_alias + 2 :]
    rows, d = x.shape
    e = gqkv.shape[1] // 6
    gain1 = small.at[:, gain : gain + d]
    sums_o[...] = sums[...]
    g1_at, b1_at, q_at, v_at, down_at = (at[i] for i in (0, 1, 2, 3, 8))
    mine = pl.multiple_of(where[Y] * 3 * e, PAIR)
    sums_o[:, q_at : q_at + e] += col_sum(gqkv[:, pl.ds(mine, e)].astype(F32))
    mine = pl.multiple_of(where[Y] * 3 * e + 2 * e, PAIR)
    sums_o[:, v_at : v_at + e] += col_sum(gqkv[:, pl.ds(mine, e)].astype(F32))
    sums_o[:, down_at : down_at + d] += col_sum(cot[...].astype(F32))
    gn1[...] = mm(gqkv[:, : 3 * e], w[0, :, 0 : 3 * e], NT) + mm(
        gqkv[:, 3 * e :], w[1, :, 0 : 3 * e], NT
    )
    for t in range(rows // PAIR):
        r = rows_of(t)
        xhat, inv = norm_stats(x[r, :].astype(F32))
        gn = gn1[r, :]
        rows_o[r, :] = (gp[r, :].astype(F32) + norm_back(gn, gain1[...], xhat, inv)).astype(BF)
        sums_o[:, g1_at : g1_at + d] += col_sum(gn * xhat)
        sums_o[:, b1_at : b1_at + d] += col_sum(gn)


def chunk_spec(shape, ch):
    return pl.BlockSpec(
        shape, lambda i: (ch,) + (0,) * (len(shape) - 1), pipeline_mode=pl.Buffered(1)
    )


def whole_spec(shape):
    return pl.BlockSpec(shape, lambda i: (0,) * len(shape), pipeline_mode=pl.Buffered(1))


SMEM_SPEC = pl.BlockSpec(memory_space=pltpu.SMEM)


def call(kernel, ch, n_ch, inputs, kept, fresh, scratch=(), name=None, mib=8):
    deps = need(name)
    in_specs, args = [], []
    for arr, kind in inputs:
        args.append(arr)
        if kind == "s":
            in_specs.append(SMEM_SPEC)
        elif kind == "c":
            in_specs.append(chunk_spec((arr.shape[0] // n_ch,) + arr.shape[1:], ch))
        else:
            in_specs.append(whole_spec(arr.shape))
    out_shapes, out_specs, aliases = [], [], {}
    for i, (shape, dtype, previous) in enumerate(kept):
        out_shapes.append(jax.ShapeDtypeStruct(shape, dtype))
        out_specs.append(chunk_spec((shape[0] // n_ch,) + shape[1:], ch))
        if previous is not None:
            aliases[len(args)] = i
            args.append(previous)
            in_specs.append(pl.BlockSpec(memory_space=pl.ANY))
    args += list(deps)
    in_specs += [pl.BlockSpec(memory_space=pl.ANY)] * len(deps)
    for shape, dtype in fresh:
        out_shapes.append(jax.ShapeDtypeStruct(shape, dtype))
        out_specs.append(whole_spec(shape))
    out = pl.pallas_call(
        functools.partial(kernel, len(aliases) + len(deps)),
        grid=(1,),
        in_specs=in_specs,
        out_specs=out_specs,
        out_shape=out_shapes,
        scratch_shapes=list(scratch),
        input_output_aliases=aliases,
        compiler_params=pltpu.CompilerParams(vmem_limit_bytes=mib * MIB),
        cost_estimate=cost(name),
        name=name.name,
    )(*args)
    return made(name, out)


WEIGHT = {
    K.grad_dn: 15,
    K.add_z_out: 2,
    K.xy_att: 15,
    K.back1: 2,
    K.finish_qkv: 40,
    K.back0: 15,
    K.a_up: 15,
    K.feed0: 15,
    K.out1: 40,
    K.add_x_dn: 40,
    K.add_z_dn: 5,
    K.add_x_qkv: 5,
    K.add_z_qkv: 15,
    K.add_c_up: 40,
    K.add_x_out: 2,
    K.add_c_out: 15,
    K.grad_qkv: 2,
}
ORDER = {
    K.gc_up: [K.y_gn2_0, K.c_dn1],
    K.back0: [K.add_c_dn],
    K.a_att: [K.p_up],
    K.z2_dn: [K.y_bias],
    K.z1_up: [K.a_dn],
    K.z2_att: [K.y_bias],
    K.add_c_up: [K.grad_dn],
    K.out0: [K.finish_dn],
    K.gc_dn: [K.y_gn2_0],
    K.xy_att: [K.z2_up],
    K.out1: [K.gz2_dn],
    K.finish_dn: [K.add_z_qkv],
    K.add_c_out: [K.gz1_up],
    K.attend0: [K.c_dn2],
    K.add_x_up: [K.grad_out],
    K.add_z_qkv: [K.add_z_up],
    K.down1: [K.gx_dn],
    K.grad_dn: [K.a_up],
    K.gc_out: [K.back0],
    K.gz2_up: [K.add_z_out],
    K.add_z_dn: [K.y_down0],
}


def cost(name):
    return pl.CostEstimate(
        flops=int(WEIGHT.get(name, 0) * 1.1e9), bytes_accessed=0, transcendentals=0
    )


MADE = {}


def need(name):
    return tuple(MADE[n] for n in ORDER.get(name, ()) if n in MADE)


def made(name, out):
    MADE[name] = out[-1] if isinstance(out, (list, tuple)) else out
    return out


def after(x, *deps):
    return lax.optimization_barrier((x,) + deps)[0] if deps else x


class Links:
    def __init__(self, n):
        self.n = n
        self.depth = n // 4
        me = lax.axis_index("dp")
        self.core, self.x, self.z = me % 2, (me // 2) % 2, me // 4
        self.y = lax.axis_index("tensor")
        self.where = jnp.stack(
            [self.z, self.x, self.core, self.y, self.z % 2, self.z // 2]
        ).astype(jnp.int32)

    def move(self, name, v, axis, pairs):
        return made(name, lax.ppermute(after(v, *need(name)), axis, pairs))

    def core_swap(self, name, v):
        return self.move(name, v, "dp", [(i, i ^ 1) for i in range(self.n)])

    def x_swap(self, name, v):
        return self.move(name, v, "dp", [(i, i ^ 2) for i in range(self.n)])

    def z_low(self, name, v):
        return self.move(name, v, "dp", [(i, i ^ 4) for i in range(self.n)])

    def z_high(self, name, v):
        return self.move(name, v, "dp", [(i, i ^ 8) for i in range(self.n)])

    def y_swap(self, name, v):
        return self.move(name, v, "tensor", [(0, 1), (1, 0)])


def simple(kernel, name, inputs, outs, **kw):
    deps = need(name)
    specs = [SMEM_SPEC if kind == "s" else whole_spec(a.shape) for a, kind in inputs]
    specs += [pl.BlockSpec(memory_space=pl.ANY)] * len(deps)
    n_in = len(inputs)

    def body(*refs):
        kernel(*refs[:n_in], *refs[n_in + len(deps) :], **kw)

    out = pl.pallas_call(
        body,
        grid=(1,),
        in_specs=specs,
        out_specs=[whole_spec(shape) for shape, _ in outs],
        out_shape=[jax.ShapeDtypeStruct(shape, dtype) for shape, dtype in outs],
        compiler_params=pltpu.CompilerParams(vmem_limit_bytes=8 * MIB),
        cost_estimate=cost(name),
        name=name.name,
    )(*[a for a, _ in inputs], *deps)
    return made(name, out)


def small_kernel(where, mine, got, *refs):
    out, row = refs[-1], [a[...].reshape(1, -1) for a in refs[:-1]]
    swap = where[3] == 0
    first, second = mine[...], got[...]
    first, second = jnp.where(swap, first, second), jnp.where(swap, second, first)
    row[2:2] = [first[0:1], second[0:1], first[1:2], second[1:2]]
    at = 0
    for a in row:
        out[:, at : at + a.shape[1]] = a
        at += a.shape[1]


def index_of(i, bit, inner):
    return (i // inner * 2 + bit) * inner + i % inner


def merge_kernel(where, own, got, out, axis, inner):
    bit = where[axis]
    if len(own.shape) == 2:
        out[bit] = own[...]
        out[1 - bit] = got[...]
        return
    for i in range(own.shape[0]):
        out[index_of(i, bit, inner)] = own[i]
        out[index_of(i, 1 - bit, inner)] = got[i]


def merge(links, name, own, got, axis, inner=1):
    shape = (2 * own.size // (own.shape[-1] * own.shape[-2]),) + own.shape[-2:]
    inputs = [(links.where, "s"), (own, "w"), (got, "w")]
    return simple(merge_kernel, name, inputs, [(shape, BF)], axis=axis, inner=inner)[0]


def grad_kernel(where, left, right, keep, send):
    n, r, width = keep.shape
    if right.shape[1] == width:
        g = mm(left[...], right[...], TN)
    else:
        mine = pl.multiple_of(where[Y] * width, PAIR)
        g = mm(left[...], right[:, pl.ds(mine, width)], TN)
    g = g.astype(BF).reshape(n, 2, r, width)
    for c in range(2):

        @pl.when(where[2] == c)
        def _(g=g, c=c):
            keep[...] = g[:, c]
            send[...] = g[:, 1 - c]


def weight_grad(links, name, left, right, width):
    deps = need(name)
    rows, d = left.shape
    n, r = links.n // 2, d // links.n
    steps = 2

    def body(*refs):
        grad_kernel(*refs[:3], *refs[3 + len(deps) :])

    out = pl.pallas_call(
        body,
        grid=(steps,),
        in_specs=[
            SMEM_SPEC,
            pl.BlockSpec((rows, d // steps), lambda i: (0, i)),
            whole_spec(right.shape),
        ]
        + [pl.BlockSpec(memory_space=pl.ANY)] * len(deps),
        out_specs=[pl.BlockSpec((n // steps, r, width), lambda i: (i, 0, 0))] * 2,
        out_shape=[jax.ShapeDtypeStruct((n, r, width), BF)] * 2,
        compiler_params=pltpu.CompilerParams(vmem_limit_bytes=20 * MIB),
        cost_estimate=cost(name),
        name=name.name,
    )(links.where, left, right, *deps)
    return made(name, out)


def halve_kernel(where, mine, got, keep, send, axis):
    bit = where[axis]
    if len(keep.shape) == 2:
        keep[...] = mine[bit].astype(F32) + got[bit].astype(F32)
        send[...] = mine[1 - bit] + got[1 - bit]
        return
    for i in range(keep.shape[0]):
        a, b = 2 * i + bit, 2 * i + 1 - bit
        keep[i] = mine[a] + got[a]
        send[i] = mine[b] + got[b]


def halve(links, name, mine, got, axis):
    n = mine.shape[0] // 2
    shape = mine.shape[1:] if n == 1 else (n,) + mine.shape[1:]
    inputs = [(links.where, "s"), (mine, "w"), (got, "w")]
    outs = [(shape, F32 if n == 1 else BF), (shape, BF)]
    return simple(halve_kernel, name, inputs, outs, axis=axis)


EXTRA = 48


def pack(v, ref, row):
    width = ref.shape[-1]
    ref[row:, :] = jnp.zeros((EXTRA, width), BF)
    for i in range(v.shape[1] // width):
        high = v[:, i * width : (i + 1) * width].astype(BF)
        low = (v[:, i * width : (i + 1) * width] - high.astype(F32)).astype(BF)
        ref[row + i : row + i + 1, :] = high
        ref[row + EXTRA // 2 + i : row + EXTRA // 2 + i + 1, :] = low


def unpack(ref, row, n):
    half = EXTRA // 2
    v = ref[row : row + half, :].astype(F32) + ref[row + half :, :].astype(F32)
    return jnp.concatenate([v[i : i + 1, :] for i in range(n)], axis=1)


def rounded(v):
    high = v.astype(BF).astype(F32)
    return high + (v - high).astype(BF).astype(F32)


def add_core_out_kernel(where, mine, got, sums, sums_got, keep, send, total):
    depth, r, _ = keep.shape
    v = sums[...] + sums_got[...]
    total[...] = rounded(v)
    for i in range(depth):
        a, b = index_of(i, where[Z_LOW], 2), index_of(i, 1 - where[Z_LOW], 2)
        keep[i] = mine[a] + got[a]
        send[i * r : (i + 1) * r, :] = mine[b] + got[b]
    pack(v, send, depth * r)


def add_core_out(links, mine, got, sums, sums_got):
    _, r, e = mine.shape
    inputs = [(links.where, "s")] + [(a, "w") for a in (mine, got, sums, sums_got)]
    outs = [((links.depth, r, e), BF), ((links.depth * r + EXTRA, e), BF), (sums.shape, F32)]
    return simple(add_core_out_kernel, K.add_c_out, inputs, outs)


def halve_sums_kernel(where, mine, got, sums, keep, send, total, axis, inner):
    bit = where[axis]
    n, r, e = mine.shape
    v = sums[...] + unpack(got, n * r, sums.shape[1] // e)
    total[...] = rounded(v)
    for i in range(n // 2):
        a, b = index_of(i, bit, inner), index_of(i, 1 - bit, inner)
        keep[i] = mine[a] + got[pl.ds(pl.multiple_of(a * r, 16), r), :]
        send[i * r : (i + 1) * r, :] = mine[b] + got[pl.ds(pl.multiple_of(b * r, 16), r), :]
    pack(v, send, n // 2 * r)


def halve_sums(links, name, mine, got, sums, axis, inner):
    n, r, e = mine.shape
    inputs = [(links.where, "s"), (mine, "w"), (got, "w"), (sums, "w")]
    outs = [((n // 2, r, e), BF), ((n // 2 * r + EXTRA, e), BF), (sums.shape, F32)]
    return simple(halve_sums_kernel, name, inputs, outs, axis=axis, inner=inner)


def finish_out_kernel(mine, got, sums, g_out, *outs, cuts, pair):
    _, r, e = mine.shape
    g_out[...] = mine[0].astype(F32) + got[0:r, :].astype(F32)
    v = sums[...] + unpack(got, r, sums.shape[1] // e)
    for i, out in enumerate(outs):
        a, b = cuts[i], cuts[i + 1]
        if i == pair:
            out[0:1, :] = v[:, a : (a + b) // 2]
            out[1:2, :] = v[:, (a + b) // 2 : b]
        else:
            out[...] = v[0, a:b]


def finish_out(links, mine, got, sums, cuts, pair):
    _, r, e = mine.shape
    sizes = [(b - a,) for a, b in zip(cuts, cuts[1:])]
    sizes[pair] = (2, sizes[pair][0] // 2)
    outs = [((r, e), F32)] + [(size, F32) for size in sizes]
    inputs = [(a, "w") for a in (mine, got, sums)]
    return simple(finish_out_kernel, K.finish_out, inputs, outs, cuts=cuts, pair=pair)


def finish_kernel(mine, got, out):
    total = mine[...] + got[...].astype(F32)
    if len(out.shape) == 3:
        e = out.shape[2]
        for t in range(3):
            out[t] = total[:, t * e : (t + 1) * e]
    else:
        out[...] = total


def finish(name, mine, got, shape):
    return simple(finish_kernel, name, [(mine, "w"), (got, "w")], [(shape, F32)])[0]


def out_kernel(bias_at, n_alias, middle, own, other, small, *refs):
    bias = small.at[:, bias_at : bias_at + middle.shape[1]]
    out = refs[n_alias]
    for t in range(middle.shape[0] // PAIR):
        r = rows_of(t)
        down = own[r, :].astype(F32) + other[r, :].astype(F32)
        out[r, :] = (middle[r, :] + (down + bias[...])).astype(BF)


def local(
    n_dp,
    patches,
    visible,
    cotangent,
    ln1_gain,
    ln1_bias,
    w_qkv,
    b_qkv,
    w_out,
    b_out,
    ln2_gain,
    ln2_bias,
    w_up,
    b_up,
    w_down,
    b_down,
):
    MADE.clear()
    samples, vis, d = patches.shape
    rows = samples * vis
    e = w_qkv.shape[2]
    f = w_up.shape[1]
    n_ch = 2
    per = rows // n_ch
    fast = n_dp == 16
    links = Links(n_dp)

    at = [0]
    for size in (d, d, e, e, d, d, d, f, d):
        at.append(at[-1] + size)
    n_sums = -(-at[-1] // e) * e
    cuts = [0, d, 2 * d, 2 * d + 2 * e] + at[5:]
    s_at = [0]
    for size in (d, d, 2 * e, 2 * e, d, d, d, f, d):
        s_at.append(s_at[-1] + size)
    b_got = links.y_swap(K.y_bias, b_qkv)
    small = simple(
        small_kernel,
        K.small,
        [(links.where, "s")]
        + [
            (a, "w")
            for a in (b_qkv, b_got, ln1_gain, ln1_bias, b_out, ln2_gain, ln2_bias, b_up, b_down)
        ],
        [((1, s_at[-1]), F32)],
    )[0]
    x = patches.reshape(rows, d)
    cot = cotangent.reshape(rows, d)
    groups = rows // PAIR * (2 * e // PAIR)

    own_att = jnp.concatenate([w_qkv[0], w_qkv[1], w_qkv[2], w_out.T], axis=1)
    own_dn = w_down.T
    if fast:
        z_att = links.z_high(K.z2_att, own_att)
        z_dn = links.z_high(K.z2_dn, own_dn)
        z_up = links.z_high(K.z2_up, w_up)
        p_att = merge(links, K.p_att, own_att, z_att, Z_HIGH)
        a_att = merge(links, K.a_att, p_att, links.z_low(K.z1_att, p_att), Z_LOW)
        x_att = links.x_swap(K.x_att, a_att)
        y_att = links.y_swap(K.y_att, a_att)
        p_dn = merge(links, K.p_dn, own_dn, z_dn, Z_HIGH)
        z_dn = links.z_low(K.z1_dn, p_dn)
        p_up = merge(links, K.p_up, w_up, z_up, Z_HIGH)
        x_up = links.x_swap(K.x_up, p_up)
        c_a = links.core_swap(K.c_att, a_att)
        a_dn = merge(links, K.a_dn, p_dn, z_dn, Z_LOW)
        x_dn = links.x_swap(K.x_dn, a_dn)
        p_up = merge(links, K.px_up, p_up, x_up, X)
        z_up = links.z_low(K.z1_up, p_up)
        c_x = links.core_swap(K.c_x_att, x_att)
        xy_att = links.y_swap(K.xy_att, x_att)
        c_y = links.core_swap(K.c_y_att, y_att)
        c_xy = links.core_swap(K.c_xy_att, xy_att)
        w_att = [(a, "w") for a in (a_att, x_att, c_a, c_x, y_att, xy_att, c_y, c_xy)]
    else:
        w_att, w_upf, w_dnf = (
            lax.all_gather(w, "dp", axis=0, tiled=True) for w in (own_att, w_up, own_dn)
        )
        w_att = [(lax.all_gather(w_att, "tensor", axis=0), "w")]
        w_feed = [(w_upf, "w"), (w_dnf, "w")]

    def attend(ch, kept, w_att):
        lays = len(w_att) > 1
        return call(
            functools.partial(attend_kernel, ch * (samples // n_ch), s_at),
            ch,
            n_ch,
            [(visible, "s"), (links.where, "s"), (x, "c"), (small, "w")] + w_att,
            [
                ((rows, d), BF, kept[0]),
                ((rows, 2 * e), BF, kept[1]),
                ((rows, 2 * e), BF, kept[2]),
                ((rows, 2 * e), BF, kept[3]),
                ((groups, PAIR, 2 * PAIR), F32, kept[4]),
                ((rows, e), BF, kept[5]),
                ((rows, d), F32, kept[6]),
                ((rows, d), BF, kept[7]),
            ],
            [((2, d, 4 * e), BF)] if lays else [],
            scratch=[pltpu.VMEM((2, per, e), BF)],
            name=(K.attend0, K.attend1)[ch],
            mib=20,
        )

    def feed(ch, kept, sums, n2, w_feed):
        lays = len(w_feed) > 2
        return call(
            functools.partial(feed_kernel, at, s_at[7], ch == 0),
            ch,
            n_ch,
            [(n2, "c"), (small, "w"), (cot, "c")] + w_feed + ([] if ch == 0 else [(sums, "w")]),
            [((rows, f), BF, kept[0]), ((rows, f), BF, kept[1])],
            [((per, d), BF), ((1, n_sums), F32)] + ([((d, f), BF)] * 2 if lays else []),
            name=(K.feed0, K.feed1)[ch],
            mib=20,
        )

    def back(ch, kept, sums):
        return call(
            functools.partial(back_kernel, at, s_at[5]),
            ch,
            n_ch,
            [
                (middle, "c"),
                (gn2[ch], "w"),
                (gn2_got[ch], "w"),
                (cot, "c"),
                (small, "w"),
                (q, "c"),
                (k, "c"),
                (v, "c"),
                (probs, "c"),
                (sums, "w"),
                (w_both, "w"),
            ],
            [((rows, d), BF, kept[0]), ((rows, 6 * e), BF, kept[1])],
            [((1, n_sums), F32)],
            scratch=[pltpu.VMEM((per, 2 * e), BF)],
            name=(K.back0, K.back1)[ch],
            mib=20,
        )

    def to_rows(ch, kept, sums):
        return call(
            functools.partial(rows_kernel, at, s_at[0]),
            ch,
            n_ch,
            [
                (links.where, "s"),
                (grad_qkv, "c"),
                (w_both, "w"),
                (x, "c"),
                (grad_proj, "c"),
                (cot, "c"),
                (small, "w"),
                (sums, "w"),
            ],
            [((rows, d), BF, kept)],
            [((1, n_sums), F32)],
            scratch=[pltpu.VMEM((per, d), F32)],
            name=(K.rows0, K.rows1)[ch],
            mib=16,
        )

    if fast:
        c_dn = [links.core_swap(K.c_dn1, a_dn), links.core_swap(K.c_dn2, x_dn)]
        a_up = merge(links, K.a_up, p_up, z_up, Z_LOW, 2)
        w_feed = [(links.where, "s"), (a_up, "w"), (links.core_swap(K.c_up, a_up), "w")]
        w_feed += [(links.where, "s")] + [(a, "w") for a in (a_dn, x_dn, *c_dn)]
    held, kept, sums = [None] * 8, [None] * 2, None
    gn2, gn2_got = [None] * n_ch, [None] * n_ch
    for ch in range(n_ch):
        held = attend(ch, held, w_att)
        if fast and ch == 0:
            *held, w_both = held
            w_att = [(w_both, "w")]
        *kept, gn2[ch], sums, a, b = list(
            feed(ch, kept, sums, held[7], w_feed)
        ) + [None] * (0 if fast and ch == 0 else 2)
        if fast and ch == 0:
            w_feed = [(a, "w"), (b, "w")]
        gn2_got[ch] = links.y_swap((K.y_gn2_0, K.y_gn2_1)[ch], gn2[ch])
    w_both = w_att[0][0]
    norm1, q, k, v, probs, mixed, middle, norm2 = held
    active, grad_up = kept
    if fast:
        k_dn, s_dn = weight_grad(links, K.grad_dn, cot, active, f)
        c_dn = links.core_swap(K.gc_dn, s_dn)
        k_up, s_up = weight_grad(links, K.grad_up, norm2, grad_up, f)
        c_up = links.core_swap(K.gc_up, s_up)
        k_dn, s_dn = halve(links, K.add_c_dn, k_dn, c_dn, X)
        x_dn = links.x_swap(K.gx_dn, s_dn)
        k_up, s_up = halve(links, K.add_c_up, k_up, c_up, X)
        x_up = links.x_swap(K.gx_up, s_up)

    kept = [None] * 2
    for ch in range(n_ch):
        *kept, sums = back(ch, kept, sums)
        if fast and ch == 0:
            k_dn, s_dn = halve(links, K.add_x_dn, k_dn, x_dn, Z_LOW)
            z_dn = links.z_low(K.gz1_dn, s_dn)
    grad_proj, grad_qkv = kept
    if fast:
        k_qkv, s_qkv = weight_grad(links, K.grad_qkv, norm1, grad_qkv, 3 * e)
        c_qkv = links.core_swap(K.gc_qkv, s_qkv)
    if fast:
        k_qkv, s_qkv = halve(links, K.add_c_qkv, k_qkv, c_qkv, X)
        x_qkv = links.x_swap(K.gx_qkv, s_qkv)
        k_out, s_out = weight_grad(links, K.grad_out, grad_proj, mixed, e)
        c_out = links.core_swap(K.gc_out, s_out)
    grad_rows = None
    down, down_got = [None] * n_ch, [None] * n_ch
    for ch in range(n_ch):
        grad_rows, sums = to_rows(ch, grad_rows, sums)
        (down[ch],) = call(
            down_kernel,
            ch,
            n_ch,
            [(active, "c"), w_feed[1]],
            [],
            [((per, d), BF)],
            name=(K.down0, K.down1)[ch],
            mib=10,
        )
        down_got[ch] = links.y_swap((K.y_down0, K.y_down1)[ch], down[ch])
        if fast and ch == 0:
            k_dn, s_dn = halve(links, K.add_z_dn, k_dn, z_dn, Z_HIGH)
            z_dn = links.z_high(K.gz2_dn, s_dn)

    if fast:
        c_sums = links.core_swap(K.c_sums, sums)
        k_up, s_up = halve(links, K.add_x_up, k_up, x_up, Z_LOW)
        z_up = links.z_low(K.gz1_up, s_up)
        k_qkv, s_qkv = halve(links, K.add_x_qkv, k_qkv, x_qkv, Z_LOW)
        z_qkv = links.z_low(K.gz1_qkv, s_qkv)
        k_out, s_out, sums = add_core_out(links, k_out, c_out, sums, c_sums)
        z_out = links.z_low(K.gz1_out, s_out)
        k_out, s_out, sums = halve_sums(links, K.add_z_out, k_out, z_out, sums, Z_HIGH, 2)
        z_out = links.z_high(K.gz2_out, s_out)
        k_up, s_up = halve(links, K.add_z_up, k_up, z_up, Z_HIGH)
        z_up = links.z_high(K.gz2_up, s_up)
        k_qkv, s_qkv = halve(links, K.add_z_qkv, k_qkv, z_qkv, Z_HIGH)
        z_qkv = links.z_high(K.gz2_qkv, s_qkv)
        k_out, s_out, sums = halve_sums(links, K.add_x_out, k_out, z_out, sums, X, 1)
        x_out = links.x_swap(K.gx_out, s_out)
        g_dn = finish(K.finish_dn, k_dn, z_dn, k_dn.shape)
        g_up = finish(K.finish_up, k_up, z_up, k_up.shape)
        g_out, *part = finish_out(links, k_out, x_out, sums, cuts, 2)
    else:
        g_dn, g_up, g_qkv, g_out = (
            lax.psum_scatter(mm(a, b, TN).astype(BF), "dp", scatter_dimension=0, tiled=True)
            for a, b in (
                (cot, active),
                (norm2, grad_up),
                (norm1, lax.dynamic_slice_in_dim(grad_qkv, links.y * 3 * e, 3 * e, axis=1)),
                (grad_proj, mixed),
            )
        )
        g_dn, g_up, g_qkv, g_out = (g.astype(F32) for g in (g_dn, g_up, g_qkv, g_out))
        g_qkv = jnp.stack([g_qkv[:, 0:e], g_qkv[:, e : 2 * e], g_qkv[:, 2 * e : 3 * e]])
        sums = lax.psum(sums, "dp")
        part = [sums[0, a:b] for a, b in zip(cuts, cuts[1:])]
        part[2] = part[2].reshape(2, e)

    output = None
    for ch in range(n_ch):
        (output,) = call(
            functools.partial(out_kernel, s_at[8]),
            ch,
            n_ch,
            [(middle, "c"), (down[ch], "w"), (down_got[ch], "w"), (small, "w")],
            [((rows, d), BF, output)],
            [],
            name=(K.out0, K.out1)[ch],
        )
    if fast:
        g_qkv = finish(K.finish_qkv, k_qkv, z_qkv, (3, k_qkv.shape[0], e))

    return (
        output.reshape(patches.shape),
        grad_rows.reshape(patches.shape),
        part[0],
        part[1],
        g_qkv,
        part[2],
        g_out.T,
        part[3],
        part[4],
        part[5],
        g_up,
        part[6],
        g_dn.T,
        part[7],
    )


def solution(mesh):
    return jax.shard_map(
        functools.partial(local, mesh.shape["dp"]),
        mesh=mesh,
        in_specs=(
            P("dp", None, None),
            P("dp"),
            P("dp", None, None),
            P(),
            P(),
            P(None, "dp", "tensor"),
            P(None, "tensor"),
            P("tensor", "dp"),
            P(),
            P(),
            P(),
            P("dp", "tensor"),
            P("tensor"),
            P("tensor", "dp"),
            P(),
        ),
        out_specs=(
            P("dp", None, None),
            P("dp", None, None),
            P(),
            P(),
            P(None, "dp", "tensor"),
            P(None, "tensor"),
            P("tensor", "dp"),
            P(),
            P(),
            P(),
            P("dp", "tensor"),
            P("tensor"),
            P("tensor", "dp"),
            P(),
        ),
        check_vma=False,
    )
```

```python
import enum
import functools

import jax
import jax.numpy as jnp
from jax import lax
from jax.experimental import pallas as pl
from jax.experimental.pallas import tpu as pltpu
from jax.sharding import PartitionSpec as P

HD = 64
VIS = 64
EPS = 1e-06
BF = jnp.bfloat16
F32 = jnp.float32
NEG = -1000000000.0
PAIR = 2 * VIS
PLACE = 6
X, Y, Z_LOW, Z_HIGH = 1, 3, 4, 5

class K(enum.Enum):
    y_bias = enum.auto()
    z2_att = enum.auto()
    z2_dn = enum.auto()
    z2_up = enum.auto()
    p_att = enum.auto()
    z1_att = enum.auto()
    a_att = enum.auto()
    x_att = enum.auto()
    y_att = enum.auto()
    p_dn = enum.auto()
    z1_dn = enum.auto()
    p_up = enum.auto()
    x_up = enum.auto()
    c_att = enum.auto()
    a_dn = enum.auto()
    x_dn = enum.auto()
    px_up = enum.auto()
    z1_up = enum.auto()
    c_x_att = enum.auto()
    xy_att = enum.auto()
    c_y_att = enum.auto()
    c_xy_att = enum.auto()
    small = enum.auto()
    c_dn1 = enum.auto()
    c_dn2 = enum.auto()
    a_up = enum.auto()
    c_up = enum.auto()
    attend0 = enum.auto()
    feed0 = enum.auto()
    y_gn2_0 = enum.auto()
    attend1 = enum.auto()
    feed1 = enum.auto()
    y_gn2_1 = enum.auto()
    grad_dn = enum.auto()
    gc_dn = enum.auto()
    grad_up = enum.auto()
    gc_up = enum.auto()
    add_c_dn = enum.auto()
    gx_dn = enum.auto()
    add_c_up = enum.auto()
    gx_up = enum.auto()
    back0 = enum.auto()
    add_x_dn = enum.auto()
    gz1_dn = enum.auto()
    back1 = enum.auto()
    grad_qkv = enum.auto()
    gc_qkv = enum.auto()
    add_c_qkv = enum.auto()
    gx_qkv = enum.auto()
    grad_out = enum.auto()
    gc_out = enum.auto()
    rows0 = enum.auto()
    down0 = enum.auto()
    y_down0 = enum.auto()
    add_z_dn = enum.auto()
    gz2_dn = enum.auto()
    rows1 = enum.auto()
    down1 = enum.auto()
    y_down1 = enum.auto()
    c_sums = enum.auto()
    add_x_up = enum.auto()
    gz1_up = enum.auto()
    add_x_qkv = enum.auto()
    gz1_qkv = enum.auto()
    add_c_out = enum.auto()
    gz1_out = enum.auto()
    add_z_out = enum.auto()
    gz2_out = enum.auto()
    add_z_up = enum.auto()
    gz2_up = enum.auto()
    add_z_qkv = enum.auto()
    gz2_qkv = enum.auto()
    add_x_out = enum.auto()
    gx_out = enum.auto()
    finish_dn = enum.auto()
    finish_up = enum.auto()
    finish_out = enum.auto()
    out0 = enum.auto()
    out1 = enum.auto()
    finish_qkv = enum.auto()


MIB = 1024 * 1024
TILE = 256

NN = (((1,), (0,)), ((), ()))
NT = (((1,), (1,)), ((), ()))
TN = (((0,), (0,)), ((), ()))


def mm(left, right, dims=NN):
    return lax.dot_general(left, right, dims, preferred_element_type=F32)


def rows_of(t):
    return pl.ds(t * PAIR, PAIR)


def tile_rows(t):
    return pl.ds(pl.multiple_of(t * PAIR, PAIR), PAIR)


def norm_stats(v):
    mean = jnp.mean(v, axis=-1, keepdims=True)
    centred = v - mean
    inv = lax.rsqrt(jnp.mean(centred * centred, axis=-1, keepdims=True) + EPS)
    return centred * inv, inv


def low_lanes(shape):
    return lax.broadcasted_iota(jnp.int32, shape, 1) < HD


def two_heads(block, low):
    zero = jnp.zeros_like(block)
    return jnp.concatenate([jnp.where(low, block, zero), jnp.where(low, zero, block)], axis=0)


def col_sum(v):
    return jnp.sum(v, axis=0, keepdims=True)


def lay_out(where, parts, buf):
    blocks, r, _ = parts[0].shape
    for b in range(blocks):
        for i, part in enumerate(parts):
            cc = where[2] if i < len(parts) // 2 else 1 - where[2]
            if len(parts) == 2:
                place = b * 2 + cc
            else:
                xx = where[1] if i % 2 == 0 else 1 - where[1]
                place = (b * 2 + xx) * 2 + cc
            buf[pl.ds(pl.multiple_of(place * r, 16), r), :] = part[b]


def attend_kernel(base, at, n_alias, counts, where, x, small, *refs):
    if len(refs[0].shape) == 3 and refs[0].dtype == BF and refs[0].shape[0] == 2:
        w, refs = refs[0], refs[1:]
        outs, (mixed,) = refs[n_alias : n_alias + 8], refs[n_alias + 8 :]
    else:
        parts, refs = refs[:8], refs[8:]
        outs, (w, mixed) = refs[n_alias : n_alias + 8], refs[n_alias + 8 :]
        lay_out(where, parts[:4], w.at[where[3]])
        lay_out(where, parts[4:], w.at[1 - where[3]])
    norm_o, q_o, k_o, v_o, probs_o, mixed_o, mid_o, norm2_o = outs
    g1, b1, b_q, b_v, b_out, g2, b2 = (small.at[:, at[i] : at[i + 1]] for i in range(7))
    rows, d = x.shape
    e = mixed_o.shape[1]
    for t in range(rows // PAIR):
        xhat, _ = norm_stats(x[rows_of(t), :].astype(F32))
        norm_o[rows_of(t), :] = (xhat * g1[...] + b1[...]).astype(BF)
    n = norm_o[...]
    for h in range(2):
        half = slice(h * e, (h + 1) * e)
        q_o[:, half] = (mm(n, w[h, :, 0:e]) + b_q[:, half]).astype(BF)
        k_o[:, half] = mm(n, w[h, :, e : 2 * e]).astype(BF)
        v_o[:, half] = (mm(n, w[h, :, 2 * e : 3 * e]) + b_v[:, half]).astype(BF)
    low = low_lanes((PAIR, PAIR))
    row = lax.broadcasted_iota(jnp.int32, (PAIR, PAIR), 0)
    col = lax.broadcasted_iota(jnp.int32, (PAIR, PAIR), 1)
    pairs = 2 * e // PAIR
    for t in range(rows // PAIR):
        first = counts[base + 2 * t]
        second = counts[base + 2 * t + 1]
        valid = ((row < VIS) & (col < jnp.minimum(first, VIS))) | (
            (row >= VIS) & (col >= VIS) & (col < VIS + second)
        )
        for p in range(pairs):
            lanes = pl.ds(p * PAIR, PAIR)
            q2 = q_o[rows_of(t), lanes]
            kc = two_heads(k_o[rows_of(t), lanes], low)
            vc = two_heads(v_o[rows_of(t), lanes], low)
            scores = mm(q2, kc, NT) * (HD**-0.5)
            for h in range(2):
                s = jnp.where(valid, scores[:, h * PAIR : (h + 1) * PAIR], NEG)
                ex = jnp.exp(s - jnp.max(s, axis=-1, keepdims=True))
                probs_o[t * pairs + p, :, pl.ds(h * PAIR, PAIR)] = ex / jnp.sum(
                    ex, axis=-1, keepdims=True
                )
            pb = probs_o[t * pairs + p].astype(BF)
            mixed[2 * p // pairs, rows_of(t), pl.ds(p % (pairs // 2) * PAIR, PAIR)] = mm(
                pb, vc
            ).astype(BF)
    mixed_o[...] = mixed[where[3]]
    for t in range(rows // PAIR):
        r = rows_of(t)
        proj = mm(mixed[0, r, :], w[0, :, 3 * e : 4 * e], NT)
        proj = proj + mm(mixed[1, r, :], w[1, :, 3 * e : 4 * e], NT)
        middle = x[r, :].astype(F32) + (proj + b_out[...])
        mid_o[r, :] = middle
        xhat, _ = norm_stats(middle)
        norm2_o[r, :] = (xhat * g2[...] + b2[...]).astype(BF)


def feed_kernel(at, up_at, first, n_alias, n2, small, cot, *refs):
    if first and refs[0].shape == (PLACE,):
        parts_up, refs = (refs[0], refs[1:3]), refs[3:]
        parts_dn, refs = (refs[0], refs[1:5]), refs[5:]
        w_up, w_dn = refs[n_alias + 4 : n_alias + 6]
        lay_out(*parts_up, w_up)
        lay_out(*parts_dn, w_dn)
    else:
        w_up, w_dn, *refs = refs
    b_up = small.at[:, up_at : up_at + w_up.shape[1]]
    if not first:
        sums, *refs = refs
    act_o, gu_o, gn_o, sums_o = refs[n_alias : n_alias + 4]
    f = w_up.shape[1]
    if first:
        sums_o[...] = jnp.zeros_like(sums_o)
    else:
        sums_o[...] = sums[...]
    for j in range(f // TILE):
        c = pl.ds(j * TILE, TILE)
        u = mm(n2[...], w_up[:, c]) + b_up[:, c]
        ga = mm(cot[...], w_dn[:, c])
        cdf = 0.5 * (1.0 + lax.erf(u * (0.5**0.5)))
        pdf = jnp.exp(u * u * -0.5) * 0.3989422804014327
        act_o[:, c] = (u * cdf).astype(BF)
        gu = (ga * (cdf + u * pdf)).astype(BF)
        gu_o[:, c] = gu
        lo = at[7] + j * TILE
        sums_o[:, lo : lo + TILE] += col_sum(gu.astype(F32))
    gn_o[...] = mm(gu_o[...], w_up[...], NT).astype(BF)


def down_kernel(n_alias, act, w_dn, *refs):
    refs[n_alias][...] = mm(act[...], w_dn[...], NT).astype(BF)


def norm_back(grad, gain, xhat, inv):
    t = grad * gain
    return inv * (
        t
        - jnp.mean(t, axis=-1, keepdims=True)
        - xhat * jnp.mean(t * xhat, axis=-1, keepdims=True)
    )


def back_kernel(at, gain, n_alias, middle, own, other, cot, small, q, k, v, probs, sums, w, *refs):
    gp_o, gqkv_o, sums_o = refs[n_alias : n_alias + 3]
    (gmix,) = refs[n_alias + 3 :]
    rows, d = cot.shape
    gain2 = small.at[:, gain : gain + d]
    e = gmix.shape[1] // 2
    sums_o[...] = sums[...]
    out_at, g2_at, b2_at = (at[i] for i in (4, 5, 6))
    for t in range(rows // PAIR):
        r = rows_of(t)
        gn = own[r, :].astype(F32) + other[r, :].astype(F32)
        xhat, inv = norm_stats(middle[r, :])
        gp = (cot[r, :].astype(F32) + norm_back(gn, gain2[...], xhat, inv)).astype(BF)
        gp_o[r, :] = gp
        sums_o[:, g2_at : g2_at + d] += col_sum(gn * xhat)
        sums_o[:, b2_at : b2_at + d] += col_sum(gn)
        sums_o[:, out_at : out_at + d] += col_sum(gp.astype(F32))
    for h in range(2):
        gmix[:, h * e : (h + 1) * e] = mm(gp_o[...], w[h, :, 3 * e : 4 * e]).astype(BF)
    low = low_lanes((PAIR, PAIR))
    pairs = 2 * e // PAIR

    @pl.loop(0, rows // PAIR)
    def _(t):
        r = tile_rows(t)
        for p in range(pairs):
            lanes = pl.ds(p * PAIR, PAIR)
            first = 2 * p // pairs * 3 * e + p % (pairs // 2) * PAIR
            q2 = q[r, lanes]
            g2 = gmix[r, lanes]
            kc = two_heads(k[r, lanes], low)
            vc = two_heads(v[r, lanes], low)
            pr = probs[t * pairs + p]
            gprob = mm(g2, vc, NT)
            halves = []
            for i in range(2):
                p_h, g_h = (a[:, i * PAIR : (i + 1) * PAIR] for a in (pr, gprob))
                row_sum = jnp.sum(p_h * g_h, axis=-1, keepdims=True)
                halves.append((p_h * (g_h - row_sum)).astype(BF))
            gs = jnp.concatenate(halves, axis=1)
            gq = mm(gs, kc) * (HD**-0.5)
            gk = mm(gs, q2, TN)
            gv = mm(pr.astype(BF), g2, TN)
            gqkv_o[r, pl.ds(first, PAIR)] = gq.astype(BF)
            gqkv_o[r, pl.ds(first + e, PAIR)] = (
                jnp.where(low, gk[:PAIR], gk[PAIR:]) * (HD**-0.5)
            ).astype(BF)
            gqkv_o[r, pl.ds(first + 2 * e, PAIR)] = jnp.where(low, gv[:PAIR], gv[PAIR:]).astype(BF)


def rows_kernel(at, gain, n_alias, where, gqkv, w, x, gp, cot, small, sums, *refs):
    rows_o, sums_o = refs[n_alias : n_alias + 2]
    (gn1,) = refs[n_alias + 2 :]
    rows, d = x.shape
    e = gqkv.shape[1] // 6
    gain1 = small.at[:, gain : gain + d]
    sums_o[...] = sums[...]
    g1_at, b1_at, q_at, v_at, down_at = (at[i] for i in (0, 1, 2, 3, 8))
    mine = pl.multiple_of(where[Y] * 3 * e, PAIR)
    sums_o[:, q_at : q_at + e] += col_sum(gqkv[:, pl.ds(mine, e)].astype(F32))
    mine = pl.multiple_of(where[Y] * 3 * e + 2 * e, PAIR)
    sums_o[:, v_at : v_at + e] += col_sum(gqkv[:, pl.ds(mine, e)].astype(F32))
    sums_o[:, down_at : down_at + d] += col_sum(cot[...].astype(F32))
    gn1[...] = mm(gqkv[:, : 3 * e], w[0, :, 0 : 3 * e], NT) + mm(
        gqkv[:, 3 * e :], w[1, :, 0 : 3 * e], NT
    )
    for t in range(rows // PAIR):
        r = rows_of(t)
        xhat, inv = norm_stats(x[r, :].astype(F32))
        gn = gn1[r, :]
        rows_o[r, :] = (gp[r, :].astype(F32) + norm_back(gn, gain1[...], xhat, inv)).astype(BF)
        sums_o[:, g1_at : g1_at + d] += col_sum(gn * xhat)
        sums_o[:, b1_at : b1_at + d] += col_sum(gn)


def chunk_spec(shape, ch):
    return pl.BlockSpec(
        shape, lambda i: (ch,) + (0,) * (len(shape) - 1), pipeline_mode=pl.Buffered(1)
    )


def whole_spec(shape):
    return pl.BlockSpec(shape, lambda i: (0,) * len(shape), pipeline_mode=pl.Buffered(1))


SMEM_SPEC = pl.BlockSpec(memory_space=pltpu.SMEM)


def call(kernel, ch, n_ch, inputs, kept, fresh, scratch=(), name=None, mib=8):
    deps = need(name)
    in_specs, args = [], []
    for arr, kind in inputs:
        args.append(arr)
        if kind == "s":
            in_specs.append(SMEM_SPEC)
        elif kind == "c":
            in_specs.append(chunk_spec((arr.shape[0] // n_ch,) + arr.shape[1:], ch))
        else:
            in_specs.append(whole_spec(arr.shape))
    out_shapes, out_specs, aliases = [], [], {}
    for i, (shape, dtype, previous) in enumerate(kept):
        out_shapes.append(jax.ShapeDtypeStruct(shape, dtype))
        out_specs.append(chunk_spec((shape[0] // n_ch,) + shape[1:], ch))
        if previous is not None:
            aliases[len(args)] = i
            args.append(previous)
            in_specs.append(pl.BlockSpec(memory_space=pl.ANY))
    args += list(deps)
    in_specs += [pl.BlockSpec(memory_space=pl.ANY)] * len(deps)
    for shape, dtype in fresh:
        out_shapes.append(jax.ShapeDtypeStruct(shape, dtype))
        out_specs.append(whole_spec(shape))
    out = pl.pallas_call(
        functools.partial(kernel, len(aliases) + len(deps)),
        grid=(1,),
        in_specs=in_specs,
        out_specs=out_specs,
        out_shape=out_shapes,
        scratch_shapes=list(scratch),
        input_output_aliases=aliases,
        compiler_params=pltpu.CompilerParams(vmem_limit_bytes=mib * MIB),
        cost_estimate=cost(name),
        name=name.name,
    )(*args)
    return made(name, out)


WEIGHT = {
    K.grad_dn: 15,
    K.add_z_out: 2,
    K.xy_att: 15,
    K.back1: 2,
    K.finish_qkv: 40,
    K.back0: 15,
    K.a_up: 15,
    K.feed0: 15,
    K.out1: 40,
    K.add_x_dn: 40,
    K.add_z_dn: 5,
    K.add_x_qkv: 5,
    K.add_z_qkv: 15,
    K.add_c_up: 40,
    K.add_x_out: 2,
    K.add_c_out: 15,
    K.grad_qkv: 2,
}
ORDER = {
    K.gc_up: [K.y_gn2_0, K.c_dn1],
    K.back0: [K.add_c_dn],
    K.a_att: [K.p_up],
    K.z2_dn: [K.y_bias],
    K.z1_up: [K.a_dn],
    K.z2_att: [K.y_bias],
    K.add_c_up: [K.grad_dn],
    K.out0: [K.finish_dn],
    K.gc_dn: [K.y_gn2_0],
    K.xy_att: [K.z2_up],
    K.out1: [K.gz2_dn],
    K.finish_dn: [K.add_z_qkv],
    K.add_c_out: [K.gz1_up],
    K.attend0: [K.c_dn2],
    K.add_x_up: [K.grad_out],
    K.add_z_qkv: [K.add_z_up],
    K.down1: [K.gx_dn],
    K.grad_dn: [K.a_up],
    K.gc_out: [K.back0],
    K.gz2_up: [K.add_z_out],
    K.add_z_dn: [K.y_down0],
}


def cost(name):
    return pl.CostEstimate(
        flops=int(WEIGHT.get(name, 0) * 1.1e9), bytes_accessed=0, transcendentals=0
    )


MADE = {}


def need(name):
    return tuple(MADE[n] for n in ORDER.get(name, ()) if n in MADE)


def made(name, out):
    MADE[name] = out[-1] if isinstance(out, (list, tuple)) else out
    return out


def after(x, *deps):
    return lax.optimization_barrier((x,) + deps)[0] if deps else x


class Links:
    def __init__(self, n):
        self.n = n
        self.depth = n // 4
        me = lax.axis_index("dp")
        self.core, self.x, self.z = me % 2, (me // 2) % 2, me // 4
        self.y = lax.axis_index("tensor")
        self.where = jnp.stack(
            [self.z, self.x, self.core, self.y, self.z % 2, self.z // 2]
        ).astype(jnp.int32)

    def move(self, name, v, axis, pairs):
        return made(name, lax.ppermute(after(v, *need(name)), axis, pairs))

    def core_swap(self, name, v):
        return self.move(name, v, "dp", [(i, i ^ 1) for i in range(self.n)])

    def x_swap(self, name, v):
        return self.move(name, v, "dp", [(i, i ^ 2) for i in range(self.n)])

    def z_low(self, name, v):
        return self.move(name, v, "dp", [(i, i ^ 4) for i in range(self.n)])

    def z_high(self, name, v):
        return self.move(name, v, "dp", [(i, i ^ 8) for i in range(self.n)])

    def y_swap(self, name, v):
        return self.move(name, v, "tensor", [(0, 1), (1, 0)])


def simple(kernel, name, inputs, outs, **kw):
    deps = need(name)
    specs = [SMEM_SPEC if kind == "s" else whole_spec(a.shape) for a, kind in inputs]
    specs += [pl.BlockSpec(memory_space=pl.ANY)] * len(deps)
    n_in = len(inputs)

    def body(*refs):
        kernel(*refs[:n_in], *refs[n_in + len(deps) :], **kw)

    out = pl.pallas_call(
        body,
        grid=(1,),
        in_specs=specs,
        out_specs=[whole_spec(shape) for shape, _ in outs],
        out_shape=[jax.ShapeDtypeStruct(shape, dtype) for shape, dtype in outs],
        compiler_params=pltpu.CompilerParams(vmem_limit_bytes=8 * MIB),
        cost_estimate=cost(name),
        name=name.name,
    )(*[a for a, _ in inputs], *deps)
    return made(name, out)


def small_kernel(where, mine, got, *refs):
    out, row = refs[-1], [a[...].reshape(1, -1) for a in refs[:-1]]
    swap = where[3] == 0
    first, second = mine[...], got[...]
    first, second = jnp.where(swap, first, second), jnp.where(swap, second, first)
    row[2:2] = [first[0:1], second[0:1], first[1:2], second[1:2]]
    at = 0
    for a in row:
        out[:, at : at + a.shape[1]] = a
        at += a.shape[1]


def index_of(i, bit, inner):
    return (i // inner * 2 + bit) * inner + i % inner


def merge_kernel(where, own, got, out, axis, inner):
    bit = where[axis]
    if len(own.shape) == 2:
        out[bit] = own[...]
        out[1 - bit] = got[...]
        return
    for i in range(own.shape[0]):
        out[index_of(i, bit, inner)] = own[i]
        out[index_of(i, 1 - bit, inner)] = got[i]


def merge(links, name, own, got, axis, inner=1):
    shape = (2 * own.size // (own.shape[-1] * own.shape[-2]),) + own.shape[-2:]
    inputs = [(links.where, "s"), (own, "w"), (got, "w")]
    return simple(merge_kernel, name, inputs, [(shape, BF)], axis=axis, inner=inner)[0]


def grad_kernel(where, left, right, keep, send):
    n, r, width = keep.shape
    if right.shape[1] == width:
        g = mm(left[...], right[...], TN)
    else:
        mine = pl.multiple_of(where[Y] * width, PAIR)
        g = mm(left[...], right[:, pl.ds(mine, width)], TN)
    g = g.astype(BF).reshape(n, 2, r, width)
    for c in range(2):

        @pl.when(where[2] == c)
        def _(g=g, c=c):
            keep[...] = g[:, c]
            send[...] = g[:, 1 - c]


def weight_grad(links, name, left, right, width):
    deps = need(name)
    rows, d = left.shape
    n, r = links.n // 2, d // links.n
    steps = 2

    def body(*refs):
        grad_kernel(*refs[:3], *refs[3 + len(deps) :])

    out = pl.pallas_call(
        body,
        grid=(steps,),
        in_specs=[
            SMEM_SPEC,
            pl.BlockSpec((rows, d // steps), lambda i: (0, i)),
            whole_spec(right.shape),
        ]
        + [pl.BlockSpec(memory_space=pl.ANY)] * len(deps),
        out_specs=[pl.BlockSpec((n // steps, r, width), lambda i: (i, 0, 0))] * 2,
        out_shape=[jax.ShapeDtypeStruct((n, r, width), BF)] * 2,
        compiler_params=pltpu.CompilerParams(vmem_limit_bytes=20 * MIB),
        cost_estimate=cost(name),
        name=name.name,
    )(links.where, left, right, *deps)
    return made(name, out)


def halve_kernel(where, mine, got, keep, send, axis):
    bit = where[axis]
    if len(keep.shape) == 2:
        keep[...] = mine[bit].astype(F32) + got[bit].astype(F32)
        send[...] = mine[1 - bit] + got[1 - bit]
        return
    for i in range(keep.shape[0]):
        a, b = 2 * i + bit, 2 * i + 1 - bit
        keep[i] = mine[a] + got[a]
        send[i] = mine[b] + got[b]


def halve(links, name, mine, got, axis):
    n = mine.shape[0] // 2
    shape = mine.shape[1:] if n == 1 else (n,) + mine.shape[1:]
    inputs = [(links.where, "s"), (mine, "w"), (got, "w")]
    outs = [(shape, F32 if n == 1 else BF), (shape, BF)]
    return simple(halve_kernel, name, inputs, outs, axis=axis)


EXTRA = 48


def pack(v, ref, row):
    width = ref.shape[-1]
    ref[row:, :] = jnp.zeros((EXTRA, width), BF)
    for i in range(v.shape[1] // width):
        high = v[:, i * width : (i + 1) * width].astype(BF)
        low = (v[:, i * width : (i + 1) * width] - high.astype(F32)).astype(BF)
        ref[row + i : row + i + 1, :] = high
        ref[row + EXTRA // 2 + i : row + EXTRA // 2 + i + 1, :] = low


def unpack(ref, row, n):
    half = EXTRA // 2
    v = ref[row : row + half, :].astype(F32) + ref[row + half :, :].astype(F32)
    return jnp.concatenate([v[i : i + 1, :] for i in range(n)], axis=1)


def rounded(v):
    high = v.astype(BF).astype(F32)
    return high + (v - high).astype(BF).astype(F32)


def add_core_out_kernel(where, mine, got, sums, sums_got, keep, send, total):
    depth, r, _ = keep.shape
    v = sums[...] + sums_got[...]
    total[...] = rounded(v)
    for i in range(depth):
        a, b = index_of(i, where[Z_LOW], 2), index_of(i, 1 - where[Z_LOW], 2)
        keep[i] = mine[a] + got[a]
        send[i * r : (i + 1) * r, :] = mine[b] + got[b]
    pack(v, send, depth * r)


def add_core_out(links, mine, got, sums, sums_got):
    _, r, e = mine.shape
    inputs = [(links.where, "s")] + [(a, "w") for a in (mine, got, sums, sums_got)]
    outs = [((links.depth, r, e), BF), ((links.depth * r + EXTRA, e), BF), (sums.shape, F32)]
    return simple(add_core_out_kernel, K.add_c_out, inputs, outs)


def halve_sums_kernel(where, mine, got, sums, keep, send, total, axis, inner):
    bit = where[axis]
    n, r, e = mine.shape
    v = sums[...] + unpack(got, n * r, sums.shape[1] // e)
    total[...] = rounded(v)
    for i in range(n // 2):
        a, b = index_of(i, bit, inner), index_of(i, 1 - bit, inner)
        keep[i] = mine[a] + got[pl.ds(pl.multiple_of(a * r, 16), r), :]
        send[i * r : (i + 1) * r, :] = mine[b] + got[pl.ds(pl.multiple_of(b * r, 16), r), :]
    pack(v, send, n // 2 * r)


def halve_sums(links, name, mine, got, sums, axis, inner):
    n, r, e = mine.shape
    inputs = [(links.where, "s"), (mine, "w"), (got, "w"), (sums, "w")]
    outs = [((n // 2, r, e), BF), ((n // 2 * r + EXTRA, e), BF), (sums.shape, F32)]
    return simple(halve_sums_kernel, name, inputs, outs, axis=axis, inner=inner)


def finish_out_kernel(mine, got, sums, g_out, *outs, cuts, pair):
    _, r, e = mine.shape
    g_out[...] = mine[0].astype(F32) + got[0:r, :].astype(F32)
    v = sums[...] + unpack(got, r, sums.shape[1] // e)
    for i, out in enumerate(outs):
        a, b = cuts[i], cuts[i + 1]
        if i == pair:
            out[0:1, :] = v[:, a : (a + b) // 2]
            out[1:2, :] = v[:, (a + b) // 2 : b]
        else:
            out[...] = v[0, a:b]


def finish_out(links, mine, got, sums, cuts, pair):
    _, r, e = mine.shape
    sizes = [(b - a,) for a, b in zip(cuts, cuts[1:])]
    sizes[pair] = (2, sizes[pair][0] // 2)
    outs = [((r, e), F32)] + [(size, F32) for size in sizes]
    inputs = [(a, "w") for a in (mine, got, sums)]
    return simple(finish_out_kernel, K.finish_out, inputs, outs, cuts=cuts, pair=pair)


def finish_kernel(mine, got, out):
    total = mine[...] + got[...].astype(F32)
    if len(out.shape) == 3:
        e = out.shape[2]
        for t in range(3):
            out[t] = total[:, t * e : (t + 1) * e]
    else:
        out[...] = total


def finish(name, mine, got, shape):
    return simple(finish_kernel, name, [(mine, "w"), (got, "w")], [(shape, F32)])[0]


def out_kernel(bias_at, n_alias, middle, own, other, small, *refs):
    bias = small.at[:, bias_at : bias_at + middle.shape[1]]
    out = refs[n_alias]
    for t in range(middle.shape[0] // PAIR):
        r = rows_of(t)
        down = own[r, :].astype(F32) + other[r, :].astype(F32)
        out[r, :] = (middle[r, :] + (down + bias[...])).astype(BF)


def local(
    n_dp,
    patches,
    visible,
    cotangent,
    ln1_gain,
    ln1_bias,
    w_qkv,
    b_qkv,
    w_out,
    b_out,
    ln2_gain,
    ln2_bias,
    w_up,
    b_up,
    w_down,
    b_down,
):
    MADE.clear()
    samples, vis, d = patches.shape
    rows = samples * vis
    e = w_qkv.shape[2]
    f = w_up.shape[1]
    n_ch = 2
    per = rows // n_ch
    fast = n_dp == 16
    links = Links(n_dp)

    at = [0]
    for size in (d, d, e, e, d, d, d, f, d):
        at.append(at[-1] + size)
    n_sums = -(-at[-1] // e) * e
    cuts = [0, d, 2 * d, 2 * d + 2 * e] + at[5:]
    s_at = [0]
    for size in (d, d, 2 * e, 2 * e, d, d, d, f, d):
        s_at.append(s_at[-1] + size)
    b_got = links.y_swap(K.y_bias, b_qkv)
    small = simple(
        small_kernel,
        K.small,
        [(links.where, "s")]
        + [
            (a, "w")
            for a in (b_qkv, b_got, ln1_gain, ln1_bias, b_out, ln2_gain, ln2_bias, b_up, b_down)
        ],
        [((1, s_at[-1]), F32)],
    )[0]
    x = patches.reshape(rows, d)
    cot = cotangent.reshape(rows, d)
    groups = rows // PAIR * (2 * e // PAIR)

    own_att = jnp.concatenate([w_qkv[0], w_qkv[1], w_qkv[2], w_out.T], axis=1)
    own_dn = w_down.T
    if fast:
        z_att = links.z_high(K.z2_att, own_att)
        z_dn = links.z_high(K.z2_dn, own_dn)
        z_up = links.z_high(K.z2_up, w_up)
        p_att = merge(links, K.p_att, own_att, z_att, Z_HIGH)
        a_att = merge(links, K.a_att, p_att, links.z_low(K.z1_att, p_att), Z_LOW)
        x_att = links.x_swap(K.x_att, a_att)
        y_att = links.y_swap(K.y_att, a_att)
        p_dn = merge(links, K.p_dn, own_dn, z_dn, Z_HIGH)
        z_dn = links.z_low(K.z1_dn, p_dn)
        p_up = merge(links, K.p_up, w_up, z_up, Z_HIGH)
        x_up = links.x_swap(K.x_up, p_up)
        c_a = links.core_swap(K.c_att, a_att)
        a_dn = merge(links, K.a_dn, p_dn, z_dn, Z_LOW)
        x_dn = links.x_swap(K.x_dn, a_dn)
        p_up = merge(links, K.px_up, p_up, x_up, X)
        z_up = links.z_low(K.z1_up, p_up)
        c_x = links.core_swap(K.c_x_att, x_att)
        xy_att = links.y_swap(K.xy_att, x_att)
        c_y = links.core_swap(K.c_y_att, y_att)
        c_xy = links.core_swap(K.c_xy_att, xy_att)
        w_att = [(a, "w") for a in (a_att, x_att, c_a, c_x, y_att, xy_att, c_y, c_xy)]
    else:
        w_att, w_upf, w_dnf = (
            lax.all_gather(w, "dp", axis=0, tiled=True) for w in (own_att, w_up, own_dn)
        )
        w_att = [(lax.all_gather(w_att, "tensor", axis=0), "w")]
        w_feed = [(w_upf, "w"), (w_dnf, "w")]

    def attend(ch, kept, w_att):
        lays = len(w_att) > 1
        return call(
            functools.partial(attend_kernel, ch * (samples // n_ch), s_at),
            ch,
            n_ch,
            [(visible, "s"), (links.where, "s"), (x, "c"), (small, "w")] + w_att,
            [
                ((rows, d), BF, kept[0]),
                ((rows, 2 * e), BF, kept[1]),
                ((rows, 2 * e), BF, kept[2]),
                ((rows, 2 * e), BF, kept[3]),
                ((groups, PAIR, 2 * PAIR), F32, kept[4]),
                ((rows, e), BF, kept[5]),
                ((rows, d), F32, kept[6]),
                ((rows, d), BF, kept[7]),
            ],
            [((2, d, 4 * e), BF)] if lays else [],
            scratch=[pltpu.VMEM((2, per, e), BF)],
            name=(K.attend0, K.attend1)[ch],
            mib=20,
        )

    def feed(ch, kept, sums, n2, w_feed):
        lays = len(w_feed) > 2
        return call(
            functools.partial(feed_kernel, at, s_at[7], ch == 0),
            ch,
            n_ch,
            [(n2, "c"), (small, "w"), (cot, "c")] + w_feed + ([] if ch == 0 else [(sums, "w")]),
            [((rows, f), BF, kept[0]), ((rows, f), BF, kept[1])],
            [((per, d), BF), ((1, n_sums), F32)] + ([((d, f), BF)] * 2 if lays else []),
            name=(K.feed0, K.feed1)[ch],
            mib=20,
        )

    def back(ch, kept, sums):
        return call(
            functools.partial(back_kernel, at, s_at[5]),
            ch,
            n_ch,
            [
                (middle, "c"),
                (gn2[ch], "w"),
                (gn2_got[ch], "w"),
                (cot, "c"),
                (small, "w"),
                (q, "c"),
                (k, "c"),
                (v, "c"),
                (probs, "c"),
                (sums, "w"),
                (w_both, "w"),
            ],
            [((rows, d), BF, kept[0]), ((rows, 6 * e), BF, kept[1])],
            [((1, n_sums), F32)],
            scratch=[pltpu.VMEM((per, 2 * e), BF)],
            name=(K.back0, K.back1)[ch],
            mib=20,
        )

    def to_rows(ch, kept, sums):
        return call(
            functools.partial(rows_kernel, at, s_at[0]),
            ch,
            n_ch,
            [
                (links.where, "s"),
                (grad_qkv, "c"),
                (w_both, "w"),
                (x, "c"),
                (grad_proj, "c"),
                (cot, "c"),
                (small, "w"),
                (sums, "w"),
            ],
            [((rows, d), BF, kept)],
            [((1, n_sums), F32)],
            scratch=[pltpu.VMEM((per, d), F32)],
            name=(K.rows0, K.rows1)[ch],
            mib=16,
        )

    if fast:
        c_dn = [links.core_swap(K.c_dn1, a_dn), links.core_swap(K.c_dn2, x_dn)]
        a_up = merge(links, K.a_up, p_up, z_up, Z_LOW, 2)
        w_feed = [(links.where, "s"), (a_up, "w"), (links.core_swap(K.c_up, a_up), "w")]
        w_feed += [(links.where, "s")] + [(a, "w") for a in (a_dn, x_dn, *c_dn)]
    held, kept, sums = [None] * 8, [None] * 2, None
    gn2, gn2_got = [None] * n_ch, [None] * n_ch
    for ch in range(n_ch):
        held = attend(ch, held, w_att)
        if fast and ch == 0:
            *held, w_both = held
            w_att = [(w_both, "w")]
        *kept, gn2[ch], sums, a, b = list(
            feed(ch, kept, sums, held[7], w_feed)
        ) + [None] * (0 if fast and ch == 0 else 2)
        if fast and ch == 0:
            w_feed = [(a, "w"), (b, "w")]
        gn2_got[ch] = links.y_swap((K.y_gn2_0, K.y_gn2_1)[ch], gn2[ch])
    w_both = w_att[0][0]
    norm1, q, k, v, probs, mixed, middle, norm2 = held
    active, grad_up = kept
    if fast:
        k_dn, s_dn = weight_grad(links, K.grad_dn, cot, active, f)
        c_dn = links.core_swap(K.gc_dn, s_dn)
        k_up, s_up = weight_grad(links, K.grad_up, norm2, grad_up, f)
        c_up = links.core_swap(K.gc_up, s_up)
        k_dn, s_dn = halve(links, K.add_c_dn, k_dn, c_dn, X)
        x_dn = links.x_swap(K.gx_dn, s_dn)
        k_up, s_up = halve(links, K.add_c_up, k_up, c_up, X)
        x_up = links.x_swap(K.gx_up, s_up)

    kept = [None] * 2
    for ch in range(n_ch):
        *kept, sums = back(ch, kept, sums)
        if fast and ch == 0:
            k_dn, s_dn = halve(links, K.add_x_dn, k_dn, x_dn, Z_LOW)
            z_dn = links.z_low(K.gz1_dn, s_dn)
    grad_proj, grad_qkv = kept
    if fast:
        k_qkv, s_qkv = weight_grad(links, K.grad_qkv, norm1, grad_qkv, 3 * e)
        c_qkv = links.core_swap(K.gc_qkv, s_qkv)
    if fast:
        k_qkv, s_qkv = halve(links, K.add_c_qkv, k_qkv, c_qkv, X)
        x_qkv = links.x_swap(K.gx_qkv, s_qkv)
        k_out, s_out = weight_grad(links, K.grad_out, grad_proj, mixed, e)
        c_out = links.core_swap(K.gc_out, s_out)
    grad_rows = None
    down, down_got = [None] * n_ch, [None] * n_ch
    for ch in range(n_ch):
        grad_rows, sums = to_rows(ch, grad_rows, sums)
        (down[ch],) = call(
            down_kernel,
            ch,
            n_ch,
            [(active, "c"), w_feed[1]],
            [],
            [((per, d), BF)],
            name=(K.down0, K.down1)[ch],
            mib=10,
        )
        down_got[ch] = links.y_swap((K.y_down0, K.y_down1)[ch], down[ch])
        if fast and ch == 0:
            k_dn, s_dn = halve(links, K.add_z_dn, k_dn, z_dn, Z_HIGH)
            z_dn = links.z_high(K.gz2_dn, s_dn)

    if fast:
        c_sums = links.core_swap(K.c_sums, sums)
        k_up, s_up = halve(links, K.add_x_up, k_up, x_up, Z_LOW)
        z_up = links.z_low(K.gz1_up, s_up)
        k_qkv, s_qkv = halve(links, K.add_x_qkv, k_qkv, x_qkv, Z_LOW)
        z_qkv = links.z_low(K.gz1_qkv, s_qkv)
        k_out, s_out, sums = add_core_out(links, k_out, c_out, sums, c_sums)
        z_out = links.z_low(K.gz1_out, s_out)
        k_out, s_out, sums = halve_sums(links, K.add_z_out, k_out, z_out, sums, Z_HIGH, 2)
        z_out = links.z_high(K.gz2_out, s_out)
        k_up, s_up = halve(links, K.add_z_up, k_up, z_up, Z_HIGH)
        z_up = links.z_high(K.gz2_up, s_up)
        k_qkv, s_qkv = halve(links, K.add_z_qkv, k_qkv, z_qkv, Z_HIGH)
        z_qkv = links.z_high(K.gz2_qkv, s_qkv)
        k_out, s_out, sums = halve_sums(links, K.add_x_out, k_out, z_out, sums, X, 1)
        x_out = links.x_swap(K.gx_out, s_out)
        g_dn = finish(K.finish_dn, k_dn, z_dn, k_dn.shape)
        g_up = finish(K.finish_up, k_up, z_up, k_up.shape)
        g_out, *part = finish_out(links, k_out, x_out, sums, cuts, 2)
    else:
        g_dn, g_up, g_qkv, g_out = (
            lax.psum_scatter(mm(a, b, TN).astype(BF), "dp", scatter_dimension=0, tiled=True)
            for a, b in (
                (cot, active),
                (norm2, grad_up),
                (norm1, lax.dynamic_slice_in_dim(grad_qkv, links.y * 3 * e, 3 * e, axis=1)),
                (grad_proj, mixed),
            )
        )
        g_dn, g_up, g_qkv, g_out = (g.astype(F32) for g in (g_dn, g_up, g_qkv, g_out))
        g_qkv = jnp.stack([g_qkv[:, 0:e], g_qkv[:, e : 2 * e], g_qkv[:, 2 * e : 3 * e]])
        sums = lax.psum(sums, "dp")
        part = [sums[0, a:b] for a, b in zip(cuts, cuts[1:])]
        part[2] = part[2].reshape(2, e)

    output = None
    for ch in range(n_ch):
        (output,) = call(
            functools.partial(out_kernel, s_at[8]),
            ch,
            n_ch,
            [(middle, "c"), (down[ch], "w"), (down_got[ch], "w"), (small, "w")],
            [((rows, d), BF, output)],
            [],
            name=(K.out0, K.out1)[ch],
        )
    if fast:
        g_qkv = finish(K.finish_qkv, k_qkv, z_qkv, (3, k_qkv.shape[0], e))

    return (
        output.reshape(patches.shape),
        grad_rows.reshape(patches.shape),
        part[0],
        part[1],
        g_qkv,
        part[2],
        g_out.T,
        part[3],
        part[4],
        part[5],
        g_up,
        part[6],
        g_dn.T,
        part[7],
    )


def solution(mesh):
    return jax.shard_map(
        functools.partial(local, mesh.shape["dp"]),
        mesh=mesh,
        in_specs=(
            P("dp", None, None),
            P("dp"),
            P("dp", None, None),
            P(),
            P(),
            P(None, "dp", "tensor"),
            P(None, "tensor"),
            P("tensor", "dp"),
            P(),
            P(),
            P(),
            P("dp", "tensor"),
            P("tensor"),
            P("tensor", "dp"),
            P(),
        ),
        out_specs=(
            P("dp", None, None),
            P("dp", None, None),
            P(),
            P(),
            P(None, "dp", "tensor"),
            P(None, "tensor"),
            P("tensor", "dp"),
            P(),
            P(),
            P(),
            P("dp", "tensor"),
            P("tensor"),
            P("tensor", "dp"),
            P(),
        ),
        check_vma=False,
    )
```
